32 devices in a mesh: seq: 8 (over y, x, core), head: 4 (over z).
Axes of the slice: x: 2, y: 2, z: 4, core: 2. Of those that a mesh axis runs over, the one named last changes fastest.
Arguments:
- queries: bfloat16 [8192, 40, 128], P(('seq', 'head')), may hold values from -6 to 6
- key_vectors: bfloat16 [8192, 40, 128], P(('seq', 'head')), may hold values from -6 to 6
- value_vectors: bfloat16 [8192, 40, 128], P(('seq', 'head')), may hold values from -6 to 6
- key_tiles: int32 [64, 10], replicated, may hold values from 0 to 63, as said below
Outputs:
- attended: bfloat16 [8192, 40, 128], P(('seq', 'head'))
The draws below stay inside these ranges and needn't reach their ends.
Inputs may be any that keep to these rules, and one draw needn't show every extreme that they name: `key_tiles`: shard s holds tiles s * 8 to (s + 1) * 8 - 1. In each list the first 2 entries are distinct tiles of the query tile's own shard, the first being the query tile itself; the other 8 are distinct tiles of other shards. Over the lists of one shard's query tiles, an owner shard at distance 1 to 4 contributes exactly 2 distinct tiles, one at a greater distance at most 1.
All inputs are finite; a program needn't handle non-finite values.
Results may differ from the reference program's by a relative error of at most 0.0048.
Values may be sent and summed in bfloat16 or wider, within the bound.
No kernel may reach another device: no remote copies, remote signals or barrier semaphores. Data moves between devices by JAX's collectives and lax.ppermute only.
A program may use at most 192 MiB of HBM per device.

```python
import math
import jax
import jax.numpy as jnp
from jax import lax

H = 40
DH = 128
TILE = 128
TILES_DEV = 8
LOCAL = 2
REM = 8
CAP = 2
NEAR = 4
KT = 10
NT = 64
TOKENS = 8192
N_SEQ = 8


def draw_queries(key, part):
    key = jax.random.fold_in(key, 3)
    return jnp.clip(jax.random.normal(key, (TOKENS, H, DH), jnp.float32), -6.0, 6.0).astype(jnp.bfloat16)


def draw_key_vectors(key, part):
    key = jax.random.fold_in(key, 5)
    return jnp.clip(jax.random.normal(key, (TOKENS, H, DH), jnp.float32), -6.0, 6.0).astype(jnp.bfloat16)


def draw_key_tiles(key, part):
    key = jax.random.fold_in(key, 11)
    key_coin, key_owner, key_local = jax.random.split(key, 3)
    shards = jnp.arange(N_SEQ, dtype=jnp.int32)
    distance = jnp.abs(shards[:, None] - shards[None, :])
    coin_flip = jax.random.randint(key_coin, (N_SEQ, N_SEQ), 0, 2)
    per_owner = jnp.where(distance == 0, 0, jnp.where(distance <= NEAR, CAP, jnp.where(distance == NEAR + 1, 1, coin_flip)))
    owner_scores = jax.random.randint(key_owner, (N_SEQ, N_SEQ, TILES_DEV), 0, 1 << 20) * TILES_DEV + jnp.arange(TILES_DEV, dtype=jnp.int32)
    shuffled = jnp.argsort(owner_scores, axis=-1)[:, :, :CAP].astype(jnp.int32)
    tile_ids = shards[None, :, None] * TILES_DEV + shuffled
    slot_ids = jnp.arange(CAP, dtype=jnp.int32)
    active = slot_ids[None, None, :] < per_owner[:, :, None]
    flat_slot = shards[None, :, None] * CAP + slot_ids[None, None, :]
    order_key = jnp.where(active, flat_slot, N_SEQ * CAP + flat_slot).reshape(N_SEQ, N_SEQ * CAP)
    ordering = jnp.argsort(order_key, axis=1)
    sorted_tiles = jnp.take_along_axis(tile_ids.reshape(N_SEQ, N_SEQ * CAP), ordering, axis=1)
    active_count = jnp.sum(active.astype(jnp.int32), axis=(1, 2))
    query_slots = jnp.arange(TILES_DEV, dtype=jnp.int32)[:, None] * REM + jnp.arange(REM, dtype=jnp.int32)[None, :]
    position = query_slots[None, :, :] % active_count[:, None, None]
    remote = jnp.take_along_axis(sorted_tiles, position.reshape(N_SEQ, TILES_DEV * REM), axis=1).reshape(N_SEQ, TILES_DEV, REM)
    local_scores = jax.random.randint(key_local, (N_SEQ, TILES_DEV, TILES_DEV), 0, 1 << 20) * TILES_DEV + jnp.arange(TILES_DEV, dtype=jnp.int32)
    diagonal = jnp.arange(TILES_DEV)[:, None] == jnp.arange(TILES_DEV)[None, :]
    local_scores = jnp.where(diagonal[None, :, :], -1, local_scores)
    local_part = jnp.argsort(local_scores, axis=-1)[:, :, :LOCAL].astype(jnp.int32) + shards[:, None, None] * TILES_DEV
    listed = jnp.concatenate([local_part, remote.astype(jnp.int32)], axis=-1)
    return listed.reshape(NT, KT).astype(jnp.int32)


def level_of(key, extent, cuts, least, top_value):
    gain, own = 1.0, jax.random.fold_in(key, 6)
    for axis_at, shards_of in cuts:
        steps = jnp.exp(jax.random.uniform(jax.random.fold_in(own, axis_at), (shards_of,), jnp.float32, least / len(cuts), top_value / len(cuts)))
        gain = gain * jnp.repeat(steps, extent[axis_at] // shards_of).reshape([-1 if axis == axis_at else 1 for axis in range(len(extent))])
    return gain


def centred(key, extent, width, limit, cuts=(), held_as=jnp.bfloat16):
    factor_of = level_of(key, extent, cuts, -0.22, 0.18) if cuts else 1.0
    result = jax.random.normal(key, extent, jnp.float32) * width * factor_of
    return jnp.minimum(jnp.maximum(result, -limit), limit).astype(held_as)


def setup_inputs(seed: int = 0) -> dict:
    key_list = jax.random.split(jax.random.key(seed), 5)
    queries = draw_queries(jax.random.fold_in(key_list[4], 71), 0)
    key_vectors = draw_key_vectors(jax.random.fold_in(key_list[4], 71), 0)
    value_vectors = centred(key_list[2], (TOKENS, H, DH), 1.0, 6.0, ((0, 32),))
    key_tiles = draw_key_tiles(jax.random.fold_in(key_list[4], 71), 0)
    return dict(queries=queries, key_vectors=key_vectors, value_vectors=value_vectors, key_tiles=key_tiles)


def reference(queries, key_vectors, value_vectors, key_tiles):
    token_count, head_count, head_size = queries.shape
    tile_count = key_tiles.shape[0]
    score_scale = 1.0 / math.sqrt(head_size)
    query_tiles = queries.reshape(tile_count, TILE, head_count, head_size)
    key_blocks = key_vectors.reshape(tile_count, TILE, head_count, head_size)
    value_blocks = value_vectors.reshape(tile_count, TILE, head_count, head_size)

    def one_tile(pair):
        query_tile, listed = pair
        gathered_keys = key_blocks[listed].reshape(-1, head_count, head_size).astype(jnp.float32)
        gathered_values = value_blocks[listed].reshape(-1, head_count, head_size).astype(jnp.float32)
        scores = jnp.einsum('qhd,khd->hqk', query_tile.astype(jnp.float32), gathered_keys)
        row_top = lax.optimization_barrier(jnp.max(scores, axis=-1, keepdims=True))
        weights = jnp.exp((scores - row_top) * score_scale)
        row_total = lax.optimization_barrier(jnp.sum(weights, axis=-1, keepdims=True))
        rounded = lax.optimization_barrier(weights.astype(jnp.bfloat16)).astype(jnp.float32)
        mixed = jnp.einsum('hqk,khd->hqd', rounded, gathered_values) / row_total
        return jnp.transpose(mixed, (1, 0, 2)).astype(jnp.bfloat16)
    attended = lax.map(one_tile, (query_tiles, key_tiles))
    return attended.reshape(token_count, head_count, head_size)
```

```python
import math

import jax
import jax.numpy as jnp
from jax import lax
from jax.experimental import pallas as pl
from jax.experimental.pallas import tpu as pltpu
from jax.sharding import PartitionSpec as P

TILE = 128
CAP = 2
CHUNKS = 2
BF16 = jnp.bfloat16
F32 = jnp.float32


def split_heads(own_heads):
    count = min(CHUNKS, own_heads)
    sizes = [own_heads // count + (i < own_heads % count) for i in range(count)]
    return [(sum(sizes[:i]), size) for i, size in enumerate(sizes)]


def row_block(rows):
    return TILE if rows % TILE == 0 else rows


def by_partner(array, here, partners, chunks):
    rows, heads, size = array.shape
    own_heads = heads // partners
    block = row_block(rows)

    def kernel(here_ref, in_ref, *refs):
        outs, turned = refs[:-1], refs[-1]
        turned[...] = jnp.swapaxes(in_ref[...], 0, 1)
        for k in range(partners):
            first = (here_ref[0] ^ k) * own_heads
            for c, (start, count) in enumerate(chunks):
                outs[k * len(chunks) + c][...] = turned[pl.ds(first + start, count)]

    parts = [count for _ in range(partners) for _, count in chunks]
    outs = pl.pallas_call(
        kernel,
        grid_spec=pltpu.PrefetchScalarGridSpec(
            num_scalar_prefetch=1,
            grid=(rows // block,),
            in_specs=[pl.BlockSpec((block, heads, size), lambda i, _: (i, 0, 0))],
            out_specs=[pl.BlockSpec((count, block, size), lambda i, _: (0, i, 0)) for count in parts],
            scratch_shapes=[pltpu.VMEM((heads, block, size), array.dtype)],
        ),
        out_shape=[jax.ShapeDtypeStruct((count, rows, size), array.dtype) for count in parts],
    )(here, array)
    return [outs[k * len(chunks) : (k + 1) * len(chunks)] for k in range(partners)]


def from_partners(pieces, here, chunks, heads):
    partners = len(pieces)
    own_heads = heads // partners
    rows, size = pieces[0][0].shape[1:]
    block = row_block(rows)

    def kernel(here_ref, *refs):
        ins, out, turned = refs[:-2], refs[-2], refs[-1]
        for k in range(partners):
            first = (here_ref[0] ^ k) * own_heads
            for c, (start, count) in enumerate(chunks):
                turned[pl.ds(first + start, count)] = ins[k * len(chunks) + c][...]
        out[...] = jnp.swapaxes(turned[...], 0, 1)

    flat = [piece for group in pieces for piece in group]
    return pl.pallas_call(
        kernel,
        grid_spec=pltpu.PrefetchScalarGridSpec(
            num_scalar_prefetch=1,
            grid=(rows // block,),
            in_specs=[pl.BlockSpec((piece.shape[0], block, size), lambda i, _: (0, i, 0)) for piece in flat],
            out_specs=pl.BlockSpec((block, heads, size), lambda i, _: (i, 0, 0)),
            scratch_shapes=[pltpu.VMEM((heads, block, size), BF16)],
        ),
        out_shape=jax.ShapeDtypeStruct((rows, heads, size), BF16),
    )(here, *flat)


def pick_tiles(pieces, picks):
    count, rows, size = pieces[0].shape
    readers = picks.shape[0]
    tiles = rows // TILE

    def kernel(pick_ref, *refs):
        ins, out, pool = refs[:-2], refs[-2], refs[-1]
        for k, piece in enumerate(ins):
            pool[k * tiles : (k + 1) * tiles] = piece[0].reshape(tiles, TILE, size)
        for reader in range(readers):
            for slot in range(CAP):
                out[reader, slot, 0] = pool[pick_ref[reader, slot]]

    return pl.pallas_call(
        kernel,
        grid_spec=pltpu.PrefetchScalarGridSpec(
            num_scalar_prefetch=1,
            grid=(count,),
            in_specs=[pl.BlockSpec((1, rows, size), lambda h, _: (h, 0, 0))] * len(pieces),
            out_specs=pl.BlockSpec((readers, CAP, 1, TILE, size), lambda h, _: (0, 0, h, 0, 0)),
            scratch_shapes=[pltpu.VMEM((len(pieces) * tiles, TILE, size), BF16)],
        ),
        out_shape=jax.ShapeDtypeStruct((readers, CAP, count, TILE, size), BF16),
    )(picks, *pieces)


def attend(queries, keys, values, far_keys, far_values, places):
    partners = len(queries)
    count, rows, size = queries[0].shape
    owners = far_keys.shape[0]
    tiles = rows // TILE
    near = partners * tiles
    listed = places.shape[1]
    factor = math.log2(math.e) / math.sqrt(size)

    def kernel(place_ref, *refs):
        q_refs, k_refs, v_refs = refs[:partners], refs[partners : 2 * partners], refs[2 * partners : 3 * partners]
        far_k, far_v = refs[3 * partners : 3 * partners + 2]
        outs = refs[3 * partners + 2 : 4 * partners + 2]
        k_pool, v_pool = refs[4 * partners + 2 :]
        for k in range(partners):
            k_pool[k * tiles : (k + 1) * tiles] = k_refs[k][0].reshape(tiles, TILE, size)
            v_pool[k * tiles : (k + 1) * tiles] = v_refs[k][0].reshape(tiles, TILE, size)
        k_pool[near:] = far_k[:, :, 0].reshape(owners * CAP, TILE, size)
        v_pool[near:] = far_v[:, :, 0].reshape(owners * CAP, TILE, size)
        for k in range(partners):
            for tile in range(tiles):
                at = pl.ds(tile * TILE, TILE)
                ids = [place_ref[k * tiles + tile, j] for j in range(listed)]
                key_rows = jnp.concatenate([k_pool[i] for i in ids], axis=0)
                scores = lax.dot_general(
                    q_refs[k][0, at, :], key_rows, (((1,), (1,)), ((), ())), preferred_element_type=F32
                )
                row_top = jnp.max(scores, axis=-1, keepdims=True)
                weights = jnp.exp2((scores - row_top) * factor)
                row_total = jnp.sum(weights, axis=-1, keepdims=True)
                value_rows = jnp.concatenate([v_pool[i] for i in ids], axis=0)
                mixed = jnp.dot(weights.astype(BF16), value_rows, preferred_element_type=F32)
                outs[k][0, at, :] = (mixed / row_total).astype(BF16)

    head_spec = pl.BlockSpec((1, rows, size), lambda h, _: (h, 0, 0))
    far_spec = pl.BlockSpec((owners, CAP, 1, TILE, size), lambda h, _: (0, 0, h, 0, 0))
    pool_size = near + owners * CAP
    pairs = count * partners * tiles * listed
    return pl.pallas_call(
        kernel,
        grid_spec=pltpu.PrefetchScalarGridSpec(
            num_scalar_prefetch=1,
            grid=(count,),
            in_specs=[head_spec] * (3 * partners) + [far_spec] * 2,
            out_specs=[head_spec] * partners,
            scratch_shapes=[pltpu.VMEM((pool_size, TILE, size), BF16)] * 2,
        ),
        out_shape=[jax.ShapeDtypeStruct((count, rows, size), BF16)] * partners,
        cost_estimate=pl.CostEstimate(
            flops=pairs * 4 * TILE * TILE * size,
            bytes_accessed=count * 2 * TILE * size * (2 * near + 2 * pool_size),
            transcendentals=pairs * TILE * TILE,
        ),
    )(places, *queries, *keys, *values, far_keys, far_values)


def plan(key_tiles, my_shard, here, shards, partners, tiles):
    shard_tiles = partners * tiles
    listed = key_tiles.shape[1]
    own = jnp.arange(shard_tiles, dtype=jnp.int32)
    place_of = ((own // tiles) ^ here) * tiles + own % tiles
    by_reader = key_tiles.reshape(shards, shard_tiles * listed)
    wanted = jnp.any(by_reader[:, :, None] == (my_shard * shard_tiles + own)[None, None, :], axis=1)
    rank = jnp.cumsum(wanted.astype(jnp.int32), axis=1) - 1
    slots = jnp.arange(CAP, dtype=jnp.int32)
    chosen = wanted[:, None, :] & (rank[:, None, :] == slots[None, :, None])
    picks = jnp.sum(jnp.where(chosen, place_of[None, None, :], 0), axis=2)
    lists = lax.dynamic_slice_in_dim(key_tiles, my_shard * shard_tiles, shard_tiles, 0)
    matches = lists[:, :, None] == jnp.arange(shards * shard_tiles, dtype=jnp.int32)[None, None, :]
    needed = jnp.any(matches, axis=(0, 1)).reshape(shards, shard_tiles)
    need_rank = jnp.cumsum(needed.astype(jnp.int32), axis=1) - 1
    far_place = shard_tiles + jnp.arange(shards, dtype=jnp.int32)[:, None] * CAP + need_rank
    is_own = (jnp.arange(shards, dtype=jnp.int32) == my_shard)[:, None]
    place = jnp.where(is_own, place_of[None, :], far_place).reshape(-1)
    places = jnp.sum(jnp.where(matches, place[None, None, :], 0), axis=2)
    places = places.reshape(partners, tiles, listed)
    order = jnp.arange(partners, dtype=jnp.int32) ^ here
    places = jnp.take(places, order, axis=0).reshape(shard_tiles, listed)
    return picks.astype(jnp.int32), places.astype(jnp.int32)


def shards(queries, key_vectors, value_vectors, key_tiles):
    partners = lax.axis_size("head")
    shard_count = lax.axis_size("seq")
    here = lax.axis_index("head").astype(jnp.int32)
    my_shard = lax.axis_index("seq").astype(jnp.int32)
    here_arg = here.reshape(1)
    rows, heads, _ = queries.shape
    chunks = split_heads(heads // partners)
    tiles = rows // TILE

    def swap(piece, k):
        return piece if k == 0 else lax.ppermute(piece, "head", [(i, i ^ k) for i in range(partners)])

    def exchange(parts, c):
        return [swap(parts[k][c], k) for k in range(partners)]

    key_parts = by_partner(key_vectors, here_arg, partners, chunks)
    value_parts = by_partner(value_vectors, here_arg, partners, chunks)
    query_parts = by_partner(queries, here_arg, partners, chunks)
    picks, places = plan(key_tiles, my_shard, here, shard_count, partners, tiles)

    ready = []
    for c in range(len(chunks)):
        keys = exchange(key_parts, c)
        far_keys = lax.all_to_all(pick_tiles(keys, picks), "seq", 0, 0, tiled=True)
        values = exchange(value_parts, c)
        far_values = lax.all_to_all(pick_tiles(values, picks), "seq", 0, 0, tiled=True)
        ready.append((keys, values, far_keys, far_values))
    asked = [exchange(query_parts, c) for c in range(len(chunks))]
    answers = []
    for c in range(len(chunks)):
        outs = attend(asked[c], *ready[c], places)
        answers.append([swap(outs[k], k) for k in range(partners)])
    return from_partners([[answers[c][k] for c in range(len(chunks))] for k in range(partners)], here_arg, chunks, heads)


def solution(mesh):
    return jax.shard_map(
        shards,
        mesh=mesh,
        in_specs=(
            P(("seq", "head"), None, None),
            P(("seq", "head"), None, None),
            P(("seq", "head"), None, None),
            P(),
        ),
        out_specs=P(("seq", "head"), None, None),
        check_vma=False,
    )
```

```python
import math

import jax
import jax.numpy as jnp
from jax import lax
from jax.experimental import pallas as pl
from jax.experimental.pallas import tpu as pltpu
from jax.sharding import PartitionSpec as P

TILE = 128
CAP = 2
CHUNKS = 2
BF16 = jnp.bfloat16
F32 = jnp.float32


def split_heads(own_heads):
    count = min(CHUNKS, own_heads)
    sizes = [own_heads // count + (i < own_heads % count) for i in range(count)]
    return [(sum(sizes[:i]), size) for i, size in enumerate(sizes)]


def row_block(rows):
    return TILE if rows % TILE == 0 else rows


def by_partner(array, here, partners, chunks):
    rows, heads, size = array.shape
    own_heads = heads // partners
    block = row_block(rows)

    def kernel(here_ref, in_ref, *refs):
        outs, turned = refs[:-1], refs[-1]
        turned[...] = jnp.swapaxes(in_ref[...], 0, 1)
        for k in range(partners):
            first = (here_ref[0] ^ k) * own_heads
            for c, (start, count) in enumerate(chunks):
                outs[k * len(chunks) + c][...] = turned[pl.ds(first + start, count)]

    parts = [count for _ in range(partners) for _, count in chunks]
    outs = pl.pallas_call(
        kernel,
        grid_spec=pltpu.PrefetchScalarGridSpec(
            num_scalar_prefetch=1,
            grid=(rows // block,),
            in_specs=[pl.BlockSpec((block, heads, size), lambda i, _: (i, 0, 0))],
            out_specs=[pl.BlockSpec((count, block, size), lambda i, _: (0, i, 0)) for count in parts],
            scratch_shapes=[pltpu.VMEM((heads, block, size), array.dtype)],
        ),
        out_shape=[jax.ShapeDtypeStruct((count, rows, size), array.dtype) for count in parts],
    )(here, array)
    return [outs[k * len(chunks) : (k + 1) * len(chunks)] for k in range(partners)]


def from_partners(pieces, here, chunks, heads):
    partners = len(pieces)
    own_heads = heads // partners
    rows, size = pieces[0][0].shape[1:]
    block = row_block(rows)

    def kernel(here_ref, *refs):
        ins, out, turned = refs[:-2], refs[-2], refs[-1]
        for k in range(partners):
            first = (here_ref[0] ^ k) * own_heads
            for c, (start, count) in enumerate(chunks):
                turned[pl.ds(first + start, count)] = ins[k * len(chunks) + c][...]
        out[...] = jnp.swapaxes(turned[...], 0, 1)

    flat = [piece for group in pieces for piece in group]
    return pl.pallas_call(
        kernel,
        grid_spec=pltpu.PrefetchScalarGridSpec(
            num_scalar_prefetch=1,
            grid=(rows // block,),
            in_specs=[pl.BlockSpec((piece.shape[0], block, size), lambda i, _: (0, i, 0)) for piece in flat],
            out_specs=pl.BlockSpec((block, heads, size), lambda i, _: (i, 0, 0)),
            scratch_shapes=[pltpu.VMEM((heads, block, size), BF16)],
        ),
        out_shape=jax.ShapeDtypeStruct((rows, heads, size), BF16),
    )(here, *flat)


def pick_tiles(keys, values, picks, groups):
    count, rows, size = keys[0].shape
    tiles = rows // TILE
    partners = len(keys)

    def kernel(pick_ref, *refs):
        ins, outs, pools = refs[: 2 * partners], refs[2 * partners : -2], refs[-2:]
        for kind, pool in enumerate(pools):
            for k in range(partners):
                pool[k * tiles : (k + 1) * tiles] = ins[kind * partners + k][0].reshape(tiles, TILE, size)
            for group, out in zip(groups, outs):
                for at, reader in enumerate(group):
                    for slot in range(CAP):
                        out[at, kind, slot, 0] = pool[pick_ref[reader, slot]]

    return pl.pallas_call(
        kernel,
        grid_spec=pltpu.PrefetchScalarGridSpec(
            num_scalar_prefetch=1,
            grid=(count,),
            in_specs=[pl.BlockSpec((1, rows, size), lambda h, _: (h, 0, 0))] * (2 * partners),
            out_specs=[
                pl.BlockSpec((len(group), 2, CAP, 1, TILE, size), lambda h, _: (0, 0, 0, h, 0, 0)) for group in groups
            ],
            scratch_shapes=[pltpu.VMEM((partners * tiles, TILE, size), BF16)] * 2,
        ),
        out_shape=[jax.ShapeDtypeStruct((len(group), 2, CAP, count, TILE, size), BF16) for group in groups],
    )(picks, *keys, *values)


def attend(queries, keys, values, far, places):
    partners = len(queries)
    count, rows, size = queries[0].shape
    far_count = len(far)
    far_tiles = [part.shape[0] * CAP for part in far]
    tiles = rows // TILE
    near = partners * tiles
    listed = places.shape[1]
    factor = math.log2(math.e) / math.sqrt(size)

    def kernel(place_ref, *refs):
        q_refs, k_refs, v_refs = refs[:partners], refs[partners : 2 * partners], refs[2 * partners : 3 * partners]
        far_refs = refs[3 * partners : 3 * partners + far_count]
        outs, (k_pool, v_pool) = refs[3 * partners + far_count : -2], refs[-2:]
        for k in range(partners):
            k_pool[k * tiles : (k + 1) * tiles] = k_refs[k][0].reshape(tiles, TILE, size)
            v_pool[k * tiles : (k + 1) * tiles] = v_refs[k][0].reshape(tiles, TILE, size)
        place = near
        for k, many in enumerate(far_tiles):
            k_pool[place : place + many] = far_refs[k][:, 0, :, 0].reshape(many, TILE, size)
            v_pool[place : place + many] = far_refs[k][:, 1, :, 0].reshape(many, TILE, size)
            place += many
        for k in range(partners):
            for tile in range(tiles):
                at = pl.ds(tile * TILE, TILE)
                ids = [place_ref[k * tiles + tile, j] for j in range(listed)]
                key_rows = jnp.concatenate([k_pool[i] for i in ids], axis=0)
                scores = lax.dot_general(
                    q_refs[k][0, at, :], key_rows, (((1,), (1,)), ((), ())), preferred_element_type=F32
                )
                row_top = jnp.max(scores, axis=-1, keepdims=True)
                weights = jnp.exp2((scores - row_top) * factor)
                row_total = jnp.sum(weights, axis=-1, keepdims=True)
                value_rows = jnp.concatenate([v_pool[i] for i in ids], axis=0)
                mixed = jnp.dot(weights.astype(BF16), value_rows, preferred_element_type=F32)
                outs[k][0, at, :] = (mixed / row_total).astype(BF16)

    head_spec = pl.BlockSpec((1, rows, size), lambda h, _: (h, 0, 0))
    far_specs = [
        pl.BlockSpec((part.shape[0], 2, CAP, 1, TILE, size), lambda h, _: (0, 0, 0, h, 0, 0)) for part in far
    ]
    pool_size = near + sum(far_tiles)
    pairs = count * partners * tiles * listed
    return pl.pallas_call(
        kernel,
        grid_spec=pltpu.PrefetchScalarGridSpec(
            num_scalar_prefetch=1,
            grid=(count,),
            in_specs=[head_spec] * (3 * partners) + far_specs,
            out_specs=[head_spec] * partners,
            scratch_shapes=[pltpu.VMEM((pool_size, TILE, size), BF16)] * 2,
        ),
        out_shape=[jax.ShapeDtypeStruct((count, rows, size), BF16)] * partners,
        cost_estimate=pl.CostEstimate(
            flops=pairs * 4 * TILE * TILE * size,
            bytes_accessed=count * 2 * TILE * size * (2 * near + 2 * pool_size),
            transcendentals=pairs * TILE * TILE,
        ),
    )(places, *queries, *keys, *values, *far)


def plan(key_tiles, my_shard, here, shards, partners, tiles, pairwise):
    shard_tiles = partners * tiles
    listed = key_tiles.shape[1]
    own = jnp.arange(shard_tiles, dtype=jnp.int32)
    place_of = ((own // tiles) ^ here) * tiles + own % tiles
    by_reader = key_tiles.reshape(shards, shard_tiles * listed)
    wanted = jnp.any(by_reader[:, :, None] == (my_shard * shard_tiles + own)[None, None, :], axis=1)
    rank = jnp.cumsum(wanted.astype(jnp.int32), axis=1) - 1
    slots = jnp.arange(CAP, dtype=jnp.int32)
    chosen = wanted[:, None, :] & (rank[:, None, :] == slots[None, :, None])
    picks = jnp.sum(jnp.where(chosen, place_of[None, None, :], 0), axis=2)
    lists = lax.dynamic_slice_in_dim(key_tiles, my_shard * shard_tiles, shard_tiles, 0)
    matches = lists[:, :, None] == jnp.arange(shards * shard_tiles, dtype=jnp.int32)[None, None, :]
    needed = jnp.any(matches, axis=(0, 1)).reshape(shards, shard_tiles)
    need_rank = jnp.cumsum(needed.astype(jnp.int32), axis=1) - 1
    far_at = jnp.arange(shards, dtype=jnp.int32)
    if pairwise:
        picks = jnp.take(picks, far_at ^ my_shard, axis=0)
        far_at = (far_at ^ my_shard) - 1
    far_place = shard_tiles + far_at[:, None] * CAP + need_rank
    is_own = (jnp.arange(shards, dtype=jnp.int32) == my_shard)[:, None]
    place = jnp.where(is_own, place_of[None, :], far_place).reshape(-1)
    places = jnp.sum(jnp.where(matches, place[None, None, :], 0), axis=2)
    places = places.reshape(partners, tiles, listed)
    order = jnp.arange(partners, dtype=jnp.int32) ^ here
    places = jnp.take(places, order, axis=0).reshape(shard_tiles, listed)
    return picks.astype(jnp.int32), places.astype(jnp.int32)


def shards(queries, key_vectors, value_vectors, key_tiles):
    partners = lax.axis_size("head")
    shard_count = lax.axis_size("seq")
    here = lax.axis_index("head").astype(jnp.int32)
    my_shard = lax.axis_index("seq").astype(jnp.int32)
    here_arg = here.reshape(1)
    rows, heads, _ = queries.shape
    chunks = split_heads(heads // partners)
    tiles = rows // TILE
    pairwise = False

    def swap(piece, k):
        return piece if k == 0 else lax.ppermute(piece, "head", [(i, i ^ k) for i in range(partners)])

    def exchange(parts, c):
        return [swap(parts[k][c], k) for k in range(partners)]

    key_parts = by_partner(key_vectors, here_arg, partners, chunks)
    value_parts = by_partner(value_vectors, here_arg, partners, chunks)
    query_parts = by_partner(queries, here_arg, partners, chunks)
    picks, places = plan(key_tiles, my_shard, here, shard_count, partners, tiles, pairwise)

    def share(keys, values):
        if not pairwise:
            sent = pick_tiles(keys, values, picks, [range(shard_count)])[0]
            return [lax.all_to_all(sent, "seq", 0, 0, tiled=True)]
        sent = pick_tiles(keys, values, picks, [[k] for k in range(1, shard_count)])
        return [
            lax.ppermute(part, "seq", [(i, i ^ k) for i in range(shard_count)]) for k, part in enumerate(sent, start=1)
        ]

    ready = []
    for c in range(len(chunks)):
        keys = exchange(key_parts, c)
        values = exchange(value_parts, c)
        ready.append((keys, values, share(keys, values)))
    asked = [exchange(query_parts, c) for c in range(len(chunks))]
    answers = []
    for c in range(len(chunks)):
        outs = attend(asked[c], *ready[c], places)
        answers.append([swap(outs[k], k) for k in range(partners)])
    return from_partners([[answers[c][k] for c in range(len(chunks))] for k in range(partners)], here_arg, chunks, heads)


def solution(mesh):
    return jax.shard_map(
        shards,
        mesh=mesh,
        in_specs=(
            P(("seq", "head"), None, None),
            P(("seq", "head"), None, None),
            P(("seq", "head"), None, None),
            P(),
        ),
        out_specs=P(("seq", "head"), None, None),
        check_vma=False,
    )
```

```python
import math

import jax
import jax.numpy as jnp
from jax import lax
from jax.experimental import pallas as pl
from jax.experimental.pallas import tpu as pltpu
from jax.sharding import PartitionSpec as P

TILE = 128
CAP = 2
CHUNKS = 2
BF16 = jnp.bfloat16
F32 = jnp.float32


def split_heads(own_heads):
    count = min(CHUNKS, own_heads)
    sizes = [own_heads // count + (i < own_heads % count) for i in range(count)]
    return [(sum(sizes[:i]), size) for i, size in enumerate(sizes)]


def row_block(rows):
    return TILE if rows % TILE == 0 else rows


def by_partner(array, here, partners, chunks):
    rows, heads, size = array.shape
    own_heads = heads // partners
    block = row_block(rows)

    def kernel(here_ref, in_ref, *refs):
        outs, turned = refs[:-1], refs[-1]
        turned[...] = jnp.swapaxes(in_ref[...], 0, 1)
        for k in range(partners):
            first = (here_ref[0] ^ k) * own_heads
            for c, (start, count) in enumerate(chunks):
                outs[k * len(chunks) + c][...] = turned[pl.ds(first + start, count)]

    parts = [count for _ in range(partners) for _, count in chunks]
    outs = pl.pallas_call(
        kernel,
        grid_spec=pltpu.PrefetchScalarGridSpec(
            num_scalar_prefetch=1,
            grid=(rows // block,),
            in_specs=[pl.BlockSpec((block, heads, size), lambda i, _: (i, 0, 0))],
            out_specs=[pl.BlockSpec((count, block, size), lambda i, _: (0, i, 0)) for count in parts],
            scratch_shapes=[pltpu.VMEM((heads, block, size), array.dtype)],
        ),
        out_shape=[jax.ShapeDtypeStruct((count, rows, size), array.dtype) for count in parts],
    )(here, array)
    return [outs[k * len(chunks) : (k + 1) * len(chunks)] for k in range(partners)]


def from_partners(pieces, here, chunks, heads):
    partners = len(pieces)
    own_heads = heads // partners
    rows, size = pieces[0][0].shape[1:]
    block = row_block(rows)

    def kernel(here_ref, *refs):
        ins, out, turned = refs[:-2], refs[-2], refs[-1]
        for k in range(partners):
            first = (here_ref[0] ^ k) * own_heads
            for c, (start, count) in enumerate(chunks):
                turned[pl.ds(first + start, count)] = ins[k * len(chunks) + c][...]
        out[...] = jnp.swapaxes(turned[...], 0, 1)

    flat = [piece for group in pieces for piece in group]
    return pl.pallas_call(
        kernel,
        grid_spec=pltpu.PrefetchScalarGridSpec(
            num_scalar_prefetch=1,
            grid=(rows // block,),
            in_specs=[pl.BlockSpec((piece.shape[0], block, size), lambda i, _: (0, i, 0)) for piece in flat],
            out_specs=pl.BlockSpec((block, heads, size), lambda i, _: (i, 0, 0)),
            scratch_shapes=[pltpu.VMEM((heads, block, size), BF16)],
        ),
        out_shape=jax.ShapeDtypeStruct((rows, heads, size), BF16),
    )(here, *flat)


def pick_tiles(pieces, picks, kind, buffer):
    count, rows, size = pieces[0].shape
    readers = picks.shape[0]
    tiles = rows // TILE
    partners = len(pieces)

    def kernel(pick_ref, *refs):
        out, pool, sems = refs[-3:]
        for k in range(partners):
            for tile in range(tiles):
                pool[k * tiles + tile] = refs[k][:, tile * TILE : (tile + 1) * TILE, :]
        copies = [
            pltpu.make_async_copy(
                pool.at[pick_ref[reader, slot]], out.at[reader, kind, slot], sems.at[reader * CAP + slot]
            )
            for reader in range(readers)
            for slot in range(CAP)
        ]
        for copy in copies:
            copy.start()
        for copy in copies:
            copy.wait()

    held = [] if buffer is None else [buffer]
    return pl.pallas_call(
        kernel,
        grid_spec=pltpu.PrefetchScalarGridSpec(
            num_scalar_prefetch=1,
            grid=(1,),
            in_specs=[pl.BlockSpec((count, rows, size), lambda i, _: (0, 0, 0))] * partners
            + [pl.BlockSpec(memory_space=pl.ANY)] * len(held),
            out_specs=pl.BlockSpec(memory_space=pl.ANY),
            scratch_shapes=[
                pltpu.VMEM((partners * tiles, count, TILE, size), BF16),
                pltpu.SemaphoreType.DMA((readers * CAP,)),
            ],
        ),
        out_shape=jax.ShapeDtypeStruct((readers, 2, CAP, count, TILE, size), BF16),
        input_output_aliases={1 + partners: 0} if held else {},
    )(picks, *pieces, *held)


def attend(queries, keys, values, far, places):
    partners = len(queries)
    count, rows, size = queries[0].shape
    far_count = len(far)
    far_tiles = [part.shape[0] * CAP for part in far]
    tiles = rows // TILE
    near = partners * tiles
    listed = places.shape[1]
    factor = math.log2(math.e) / math.sqrt(size)

    def kernel(place_ref, *refs):
        q_refs, k_refs, v_refs = refs[:partners], refs[partners : 2 * partners], refs[2 * partners : 3 * partners]
        far_refs = refs[3 * partners : 3 * partners + far_count]
        outs, (k_pool, v_pool) = refs[3 * partners + far_count : -2], refs[-2:]
        for k in range(partners):
            k_pool[k * tiles : (k + 1) * tiles] = k_refs[k][0].reshape(tiles, TILE, size)
            v_pool[k * tiles : (k + 1) * tiles] = v_refs[k][0].reshape(tiles, TILE, size)
        place = near
        for k, many in enumerate(far_tiles):
            k_pool[place : place + many] = far_refs[k][:, 0, :, 0].reshape(many, TILE, size)
            v_pool[place : place + many] = far_refs[k][:, 1, :, 0].reshape(many, TILE, size)
            place += many
        for k in range(partners):
            for tile in range(tiles):
                at = pl.ds(tile * TILE, TILE)
                ids = [place_ref[k * tiles + tile, j] for j in range(listed)]
                key_rows = jnp.concatenate([k_pool[i] for i in ids], axis=0)
                scores = lax.dot_general(
                    q_refs[k][0, at, :], key_rows, (((1,), (1,)), ((), ())), preferred_element_type=F32
                )
                row_top = jnp.max(scores, axis=-1, keepdims=True)
                weights = jnp.exp2((scores - row_top) * factor)
                row_total = jnp.sum(weights, axis=-1, keepdims=True)
                value_rows = jnp.concatenate([v_pool[i] for i in ids], axis=0)
                mixed = jnp.dot(weights.astype(BF16), value_rows, preferred_element_type=F32)
                outs[k][0, at, :] = (mixed / row_total).astype(BF16)

    head_spec = pl.BlockSpec((1, rows, size), lambda h, _: (h, 0, 0))
    far_specs = [
        pl.BlockSpec((part.shape[0], 2, CAP, 1, TILE, size), lambda h, _: (0, 0, 0, h, 0, 0)) for part in far
    ]
    pool_size = near + sum(far_tiles)
    pairs = count * partners * tiles * listed
    return pl.pallas_call(
        kernel,
        grid_spec=pltpu.PrefetchScalarGridSpec(
            num_scalar_prefetch=1,
            grid=(count,),
            in_specs=[head_spec] * (3 * partners) + far_specs,
            out_specs=[head_spec] * partners,
            scratch_shapes=[pltpu.VMEM((pool_size, TILE, size), BF16)] * 2,
        ),
        out_shape=[jax.ShapeDtypeStruct((count, rows, size), BF16)] * partners,
        cost_estimate=pl.CostEstimate(
            flops=pairs * 4 * TILE * TILE * size,
            bytes_accessed=count * 2 * TILE * size * (2 * near + 2 * pool_size),
            transcendentals=pairs * TILE * TILE,
        ),
    )(places, *queries, *keys, *values, *far)


def plan(key_tiles, my_shard, here, shards, partners, tiles):
    shard_tiles = partners * tiles
    listed = key_tiles.shape[1]
    own = jnp.arange(shard_tiles, dtype=jnp.int32)
    place_of = ((own // tiles) ^ here) * tiles + own % tiles
    by_reader = key_tiles.reshape(shards, shard_tiles * listed)
    wanted = jnp.any(by_reader[:, :, None] == (my_shard * shard_tiles + own)[None, None, :], axis=1)
    rank = jnp.cumsum(wanted.astype(jnp.int32), axis=1) - 1
    slots = jnp.arange(CAP, dtype=jnp.int32)
    chosen = wanted[:, None, :] & (rank[:, None, :] == slots[None, :, None])
    picks = jnp.sum(jnp.where(chosen, place_of[None, None, :], 0), axis=2)
    lists = lax.dynamic_slice_in_dim(key_tiles, my_shard * shard_tiles, shard_tiles, 0)
    matches = lists[:, :, None] == jnp.arange(shards * shard_tiles, dtype=jnp.int32)[None, None, :]
    needed = jnp.any(matches, axis=(0, 1)).reshape(shards, shard_tiles)
    need_rank = jnp.cumsum(needed.astype(jnp.int32), axis=1) - 1
    far_at = jnp.arange(shards, dtype=jnp.int32)
    far_place = shard_tiles + far_at[:, None] * CAP + need_rank
    is_own = (jnp.arange(shards, dtype=jnp.int32) == my_shard)[:, None]
    place = jnp.where(is_own, place_of[None, :], far_place).reshape(-1)
    places = jnp.sum(jnp.where(matches, place[None, None, :], 0), axis=2)
    places = places.reshape(partners, tiles, listed)
    order = jnp.arange(partners, dtype=jnp.int32) ^ here
    places = jnp.take(places, order, axis=0).reshape(shard_tiles, listed)
    return picks.astype(jnp.int32), places.astype(jnp.int32)


def shards(queries, key_vectors, value_vectors, key_tiles):
    partners = lax.axis_size("head")
    shard_count = lax.axis_size("seq")
    here = lax.axis_index("head").astype(jnp.int32)
    my_shard = lax.axis_index("seq").astype(jnp.int32)
    here_arg = here.reshape(1)
    rows, heads, _ = queries.shape
    chunks = split_heads(heads // partners)
    tiles = rows // TILE

    def swap(piece, k):
        return piece if k == 0 else lax.ppermute(piece, "head", [(i, i ^ k) for i in range(partners)])

    def exchange(parts, c):
        return [swap(parts[k][c], k) for k in range(partners)]

    key_parts = by_partner(key_vectors, here_arg, partners, chunks)
    value_parts = by_partner(value_vectors, here_arg, partners, chunks)
    query_parts = by_partner(queries, here_arg, partners, chunks)
    picks, places = plan(key_tiles, my_shard, here, shard_count, partners, tiles)

    def share(keys, values):
        sent = pick_tiles(values, picks, 1, pick_tiles(keys, picks, 0, None))
        return [lax.all_to_all(sent, "seq", 0, 0, tiled=True)]

    picks, query_parts = lax.optimization_barrier((picks, query_parts))
    ready = []
    for c in range(len(chunks)):
        keys = exchange(key_parts, c)
        values = exchange(value_parts, c)
        ready.append((keys, values, share(keys, values)))
    asked = [exchange(query_parts, c) for c in range(len(chunks))]
    answers = []
    for c in range(len(chunks)):
        outs = attend(asked[c], *ready[c], places)
        answers.append([swap(outs[k], k) for k in range(partners)])
    return from_partners([[answers[c][k] for c in range(len(chunks))] for k in range(partners)], here_arg, chunks, heads)


def solution(mesh):
    return jax.shard_map(
        shards,
        mesh=mesh,
        in_specs=(
            P(("seq", "head"), None, None),
            P(("seq", "head"), None, None),
            P(("seq", "head"), None, None),
            P(),
        ),
        out_specs=P(("seq", "head"), None, None),
        check_vma=False,
    )
```

```python
import math

import jax
import jax.numpy as jnp
from jax import lax
from jax.experimental import pallas as pl
from jax.experimental.pallas import tpu as pltpu
from jax.sharding import PartitionSpec as P

TILE = 128
CAP = 2
CHUNKS = 2
BF16 = jnp.bfloat16
F32 = jnp.float32


def split_heads(own_heads):
    count = min(CHUNKS, own_heads)
    sizes = [own_heads // count + (i < own_heads % count) for i in range(count)]
    return [(sum(sizes[:i]), size) for i, size in enumerate(sizes)]


def row_block(rows):
    return TILE if rows % TILE == 0 else rows


def by_partner(array, here, partners, chunks):
    rows, heads, size = array.shape
    own_heads = heads // partners
    block = row_block(rows)

    def kernel(here_ref, in_ref, *refs):
        outs, turned = refs[:-1], refs[-1]
        turned[...] = jnp.swapaxes(in_ref[...], 0, 1)
        for k in range(partners):
            first = (here_ref[0] ^ k) * own_heads
            for c, (start, count) in enumerate(chunks):
                outs[k * len(chunks) + c][...] = turned[pl.ds(first + start, count)]

    parts = [count for _ in range(partners) for _, count in chunks]
    outs = pl.pallas_call(
        kernel,
        grid_spec=pltpu.PrefetchScalarGridSpec(
            num_scalar_prefetch=1,
            grid=(rows // block,),
            in_specs=[pl.BlockSpec((block, heads, size), lambda i, _: (i, 0, 0))],
            out_specs=[pl.BlockSpec((count, block, size), lambda i, _: (0, i, 0)) for count in parts],
            scratch_shapes=[pltpu.VMEM((heads, block, size), array.dtype)],
        ),
        out_shape=[jax.ShapeDtypeStruct((count, rows, size), array.dtype) for count in parts],
    )(here, array)
    return [outs[k * len(chunks) : (k + 1) * len(chunks)] for k in range(partners)]


def from_partners(pieces, here, chunks, heads):
    partners = len(pieces)
    own_heads = heads // partners
    rows, size = pieces[0][0].shape[1:]
    block = row_block(rows)

    def kernel(here_ref, *refs):
        ins, out, turned = refs[:-2], refs[-2], refs[-1]
        for k in range(partners):
            first = (here_ref[0] ^ k) * own_heads
            for c, (start, count) in enumerate(chunks):
                turned[pl.ds(first + start, count)] = ins[k * len(chunks) + c][...]
        out[...] = jnp.swapaxes(turned[...], 0, 1)

    flat = [piece for group in pieces for piece in group]
    return pl.pallas_call(
        kernel,
        grid_spec=pltpu.PrefetchScalarGridSpec(
            num_scalar_prefetch=1,
            grid=(rows // block,),
            in_specs=[pl.BlockSpec((piece.shape[0], block, size), lambda i, _: (0, i, 0)) for piece in flat],
            out_specs=pl.BlockSpec((block, heads, size), lambda i, _: (i, 0, 0)),
            scratch_shapes=[pltpu.VMEM((heads, block, size), BF16)],
        ),
        out_shape=jax.ShapeDtypeStruct((rows, heads, size), BF16),
    )(here, *flat)


def pick_tiles(pieces, picks, kind, buffer):
    count, rows, size = pieces[0].shape
    readers = picks.shape[0]
    tiles = rows // TILE
    partners = len(pieces)

    def kernel(pick_ref, *refs):
        ins = refs[:partners]
        out, sems = refs[-2:]

        def copy_of(k, row, reader, slot):
            source = ins[k].at[:, pl.ds(row, TILE), :]
            return pltpu.make_async_copy(source, out.at[reader, kind, slot], sems.at[reader * CAP + slot])

        wanted = [(reader, slot) for reader in range(readers) for slot in range(CAP)]
        for reader, slot in wanted:
            place = pick_ref[reader, slot]
            row = pl.multiple_of(lax.rem(place, tiles) * TILE, TILE)
            for k in range(partners):

                @pl.when(lax.div(place, tiles) == k)
                def _(k=k, row=row, reader=reader, slot=slot):
                    copy_of(k, row, reader, slot).start()

        for reader, slot in wanted:
            copy_of(0, 0, reader, slot).wait()

    held = [] if buffer is None else [buffer]
    return pl.pallas_call(
        kernel,
        in_specs=[pl.BlockSpec(memory_space=pltpu.SMEM)]
        + [pl.BlockSpec(memory_space=pl.ANY)] * partners
        + [pl.BlockSpec(memory_space=pltpu.HBM)] * len(held),
        out_specs=pl.BlockSpec(memory_space=pltpu.HBM),
        scratch_shapes=[pltpu.SemaphoreType.DMA((readers * CAP,))],
        out_shape=jax.ShapeDtypeStruct((readers, 2, CAP, count, TILE, size), BF16),
        input_output_aliases={1 + partners: 0} if held else {},
        compiler_params=pltpu.CompilerParams(vmem_limit_bytes=50 * 2**20),
    )(picks, *pieces, *held)


def attend(queries, keys, values, far, places):
    partners = len(queries)
    count, rows, size = queries[0].shape
    far_count = len(far)
    far_tiles = [part.shape[0] * CAP for part in far]
    tiles = rows // TILE
    near = partners * tiles
    listed = places.shape[1]
    factor = math.log2(math.e) / math.sqrt(size)

    def kernel(place_ref, *refs):
        q_refs, k_refs, v_refs = refs[:partners], refs[partners : 2 * partners], refs[2 * partners : 3 * partners]
        far_refs = refs[3 * partners : 3 * partners + far_count]
        outs, (k_pool, v_pool) = refs[3 * partners + far_count : -2], refs[-2:]
        for k in range(partners):
            k_pool[k * tiles : (k + 1) * tiles] = k_refs[k][0].reshape(tiles, TILE, size)
            v_pool[k * tiles : (k + 1) * tiles] = v_refs[k][0].reshape(tiles, TILE, size)
        place = near
        for k, many in enumerate(far_tiles):
            k_pool[place : place + many] = far_refs[k][:, 0, :, 0].reshape(many, TILE, size)
            v_pool[place : place + many] = far_refs[k][:, 1, :, 0].reshape(many, TILE, size)
            place += many
        for k in range(partners):
            for tile in range(tiles):
                at = pl.ds(tile * TILE, TILE)
                ids = [place_ref[k * tiles + tile, j] for j in range(listed)]
                key_rows = jnp.concatenate([k_pool[i] for i in ids], axis=0)
                scores = lax.dot_general(
                    q_refs[k][0, at, :], key_rows, (((1,), (1,)), ((), ())), preferred_element_type=F32
                )
                row_top = jnp.max(scores, axis=-1, keepdims=True)
                weights = jnp.exp2((scores - row_top) * factor)
                value_rows = jnp.concatenate([v_pool[i] for i in ids], axis=0)
                beside = jnp.concatenate([value_rows, jnp.ones_like(value_rows)], axis=1)
                mixed = jnp.dot(weights.astype(BF16), beside, preferred_element_type=F32)
                outs[k][0, at, :] = (mixed[:, :size] / mixed[:, size:]).astype(BF16)

    head_spec = pl.BlockSpec((1, rows, size), lambda h, _: (h, 0, 0))
    far_specs = [
        pl.BlockSpec((part.shape[0], 2, CAP, 1, TILE, size), lambda h, _: (0, 0, 0, h, 0, 0)) for part in far
    ]
    pool_size = near + sum(far_tiles)
    pairs = count * partners * tiles * listed
    return pl.pallas_call(
        kernel,
        grid_spec=pltpu.PrefetchScalarGridSpec(
            num_scalar_prefetch=1,
            grid=(count,),
            in_specs=[head_spec] * (3 * partners) + far_specs,
            out_specs=[head_spec] * partners,
            scratch_shapes=[pltpu.VMEM((pool_size, TILE, size), BF16)] * 2,
        ),
        out_shape=[jax.ShapeDtypeStruct((count, rows, size), BF16)] * partners,
        cost_estimate=pl.CostEstimate(
            flops=pairs * 4 * TILE * TILE * size,
            bytes_accessed=count * 2 * TILE * size * (2 * near + 2 * pool_size),
            transcendentals=pairs * TILE * TILE,
        ),
    )(places, *queries, *keys, *values, *far)


def plan(key_tiles, my_shard, here, shards, partners, tiles):
    shard_tiles = partners * tiles
    listed = key_tiles.shape[1]
    own = jnp.arange(shard_tiles, dtype=jnp.int32)
    place_of = ((own // tiles) ^ here) * tiles + own % tiles
    by_reader = key_tiles.reshape(shards, shard_tiles * listed)
    wanted = jnp.any(by_reader[:, :, None] == (my_shard * shard_tiles + own)[None, None, :], axis=1)
    rank = jnp.cumsum(wanted.astype(jnp.int32), axis=1) - 1
    slots = jnp.arange(CAP, dtype=jnp.int32)
    chosen = wanted[:, None, :] & (rank[:, None, :] == slots[None, :, None])
    picks = jnp.sum(jnp.where(chosen, place_of[None, None, :], 0), axis=2)
    lists = lax.dynamic_slice_in_dim(key_tiles, my_shard * shard_tiles, shard_tiles, 0)
    matches = lists[:, :, None] == jnp.arange(shards * shard_tiles, dtype=jnp.int32)[None, None, :]
    needed = jnp.any(matches, axis=(0, 1)).reshape(shards, shard_tiles)
    need_rank = jnp.cumsum(needed.astype(jnp.int32), axis=1) - 1
    far_at = jnp.arange(shards, dtype=jnp.int32)
    far_place = shard_tiles + far_at[:, None] * CAP + need_rank
    is_own = (jnp.arange(shards, dtype=jnp.int32) == my_shard)[:, None]
    place = jnp.where(is_own, place_of[None, :], far_place).reshape(-1)
    places = jnp.sum(jnp.where(matches, place[None, None, :], 0), axis=2)
    places = places.reshape(partners, tiles, listed)
    order = jnp.arange(partners, dtype=jnp.int32) ^ here
    places = jnp.take(places, order, axis=0).reshape(shard_tiles, listed)
    return picks.astype(jnp.int32), places.astype(jnp.int32)


def shards(queries, key_vectors, value_vectors, key_tiles):
    partners = lax.axis_size("head")
    shard_count = lax.axis_size("seq")
    here = lax.axis_index("head").astype(jnp.int32)
    my_shard = lax.axis_index("seq").astype(jnp.int32)
    here_arg = here.reshape(1)
    rows, heads, _ = queries.shape
    chunks = split_heads(heads // partners)
    tiles = rows // TILE

    def swap(piece, k):
        return piece if k == 0 else lax.ppermute(piece, "head", [(i, i ^ k) for i in range(partners)])

    def exchange(parts, c):
        return [swap(parts[k][c], k) for k in range(partners)]

    key_parts = by_partner(key_vectors, here_arg, partners, chunks)
    value_parts = by_partner(value_vectors, here_arg, partners, chunks)
    query_parts = by_partner(queries, here_arg, partners, chunks)
    picks, places = plan(key_tiles, my_shard, here, shard_count, partners, tiles)

    def share(keys, values):
        sent = pick_tiles(values, picks, 1, pick_tiles(keys, picks, 0, None))
        return [lax.all_to_all(sent, "seq", 0, 0, tiled=True)]

    picks, query_parts = lax.optimization_barrier((picks, query_parts))
    ready = []
    for c in range(len(chunks)):
        keys = exchange(key_parts, c)
        values = exchange(value_parts, c)
        ready.append((keys, values, share(keys, values)))
    asked = [exchange(query_parts, c) for c in range(len(chunks))]
    answers = []
    for c in range(len(chunks)):
        outs, _ = lax.optimization_barrier((attend(asked[c], *ready[c], places), [pieces[2] for pieces in asked]))
        answers.append([swap(outs[k], k) for k in range(partners)])
    return from_partners([[answers[c][k] for c in range(len(chunks))] for k in range(partners)], here_arg, chunks, heads)


def solution(mesh):
    return jax.shard_map(
        shards,
        mesh=mesh,
        in_specs=(
            P(("seq", "head"), None, None),
            P(("seq", "head"), None, None),
            P(("seq", "head"), None, None),
            P(),
        ),
        out_specs=P(("seq", "head"), None, None),
        check_vma=False,
    )
```

```python
import math

import jax
import jax.numpy as jnp
from jax import lax
from jax.experimental import pallas as pl
from jax.experimental.pallas import tpu as pltpu
from jax.sharding import PartitionSpec as P

TILE = 128
CAP = 2
CHUNKS = 2
BF16 = jnp.bfloat16
F32 = jnp.float32


def split_heads(own_heads):
    count = min(CHUNKS, own_heads)
    sizes = [own_heads // count + (i < own_heads % count) for i in range(count)]
    return [(sum(sizes[:i]), size) for i, size in enumerate(sizes)]


def row_block(rows):
    return TILE if rows % TILE == 0 else rows


def by_partner(array, here, partners, chunks):
    rows, heads, size = array.shape
    own_heads = heads // partners
    block = row_block(rows)

    def kernel(here_ref, in_ref, *refs):
        outs, turned = refs[:-1], refs[-1]
        turned[...] = jnp.swapaxes(in_ref[...], 0, 1)
        for k in range(partners):
            first = (here_ref[0] ^ k) * own_heads
            for c, (start, count) in enumerate(chunks):
                outs[k * len(chunks) + c][...] = turned[pl.ds(first + start, count)]

    parts = [count for _ in range(partners) for _, count in chunks]
    outs = pl.pallas_call(
        kernel,
        grid_spec=pltpu.PrefetchScalarGridSpec(
            num_scalar_prefetch=1,
            grid=(rows // block,),
            in_specs=[pl.BlockSpec((block, heads, size), lambda i, _: (i, 0, 0))],
            out_specs=[pl.BlockSpec((count, block, size), lambda i, _: (0, i, 0)) for count in parts],
            scratch_shapes=[pltpu.VMEM((heads, block, size), array.dtype)],
        ),
        out_shape=[jax.ShapeDtypeStruct((count, rows, size), array.dtype) for count in parts],
    )(here, array)
    return [outs[k * len(chunks) : (k + 1) * len(chunks)] for k in range(partners)]


def from_partners(pieces, here, chunks, heads):
    partners = len(pieces)
    own_heads = heads // partners
    rows, size = pieces[0][0].shape[1:]
    block = row_block(rows)

    def kernel(here_ref, *refs):
        ins, out, turned = refs[:-2], refs[-2], refs[-1]
        for k in range(partners):
            first = (here_ref[0] ^ k) * own_heads
            for c, (start, count) in enumerate(chunks):
                turned[pl.ds(first + start, count)] = ins[k * len(chunks) + c][...]
        out[...] = jnp.swapaxes(turned[...], 0, 1)

    flat = [piece for group in pieces for piece in group]
    return pl.pallas_call(
        kernel,
        grid_spec=pltpu.PrefetchScalarGridSpec(
            num_scalar_prefetch=1,
            grid=(rows // block,),
            in_specs=[pl.BlockSpec((piece.shape[0], block, size), lambda i, _: (0, i, 0)) for piece in flat],
            out_specs=pl.BlockSpec((block, heads, size), lambda i, _: (i, 0, 0)),
            scratch_shapes=[pltpu.VMEM((heads, block, size), BF16)],
        ),
        out_shape=jax.ShapeDtypeStruct((rows, heads, size), BF16),
        compiler_params=pltpu.CompilerParams(vmem_limit_bytes=16 * 2**20),
    )(here, *flat)


def pick_tiles(pieces, picks, kind, buffer):
    count, rows, size = pieces[0].shape
    readers = picks.shape[0]
    tiles = rows // TILE
    partners = len(pieces)

    def kernel(pick_ref, *refs):
        ins = refs[:partners][::-1]
        out, sems = refs[-2:]

        def copy_of(k, row, reader, slot):
            source = ins[k].at[:, pl.ds(row, TILE), :]
            return pltpu.make_async_copy(source, out.at[reader, kind, slot], sems.at[reader * CAP + slot])

        wanted = [(reader, slot) for reader in range(readers) for slot in range(CAP)]
        for reader, slot in wanted:
            place = pick_ref[reader, slot]
            row = pl.multiple_of(lax.rem(place, tiles) * TILE, TILE)
            for k in range(partners):

                @pl.when(lax.div(place, tiles) == k)
                def _(k=k, row=row, reader=reader, slot=slot):
                    copy_of(k, row, reader, slot).start()

        for reader, slot in wanted:
            copy_of(0, 0, reader, slot).wait()

    held = [] if buffer is None else [buffer]
    return pl.pallas_call(
        kernel,
        in_specs=[pl.BlockSpec(memory_space=pltpu.SMEM)]
        + [pl.BlockSpec(memory_space=pl.ANY)] * partners
        + [pl.BlockSpec(memory_space=pltpu.HBM)] * len(held),
        out_specs=pl.BlockSpec(memory_space=pltpu.HBM),
        scratch_shapes=[pltpu.SemaphoreType.DMA((readers * CAP,))],
        out_shape=jax.ShapeDtypeStruct((readers, 2, CAP, count, TILE, size), BF16),
        input_output_aliases={1 + partners: 0} if held else {},
        compiler_params=pltpu.CompilerParams(vmem_limit_bytes=50 * 2**20),
    )(picks, *pieces[::-1], *held)


def attend(queries, keys, values, far, places, turn):
    partners = len(queries)
    count, rows, size = queries[0].shape
    far_count = len(far)
    far_tiles = [part.shape[0] * CAP for part in far]
    tiles = rows // TILE
    near = partners * tiles
    listed = places.shape[1]
    factor = math.log2(math.e) / math.sqrt(size)

    def kernel(place_ref, *refs):
        q_refs = refs[:partners][::turn]
        k_refs, v_refs = refs[partners : 2 * partners][::-1], refs[2 * partners : 3 * partners]
        far_refs = refs[3 * partners : 3 * partners + far_count]
        outs, (k_pool, v_pool) = refs[3 * partners + far_count : -2], refs[-2:]
        for k in range(partners):
            k_pool[k * tiles : (k + 1) * tiles] = k_refs[k][0].reshape(tiles, TILE, size)
            v_pool[k * tiles : (k + 1) * tiles] = v_refs[k][0].reshape(tiles, TILE, size)
        place = near
        for k, many in enumerate(far_tiles):
            k_pool[place : place + many] = far_refs[k][:, 0, :, 0].reshape(many, TILE, size)
            v_pool[place : place + many] = far_refs[k][:, 1, :, 0].reshape(many, TILE, size)
            place += many
        for k in range(partners):
            for tile in range(tiles):
                at = pl.ds(tile * TILE, TILE)
                ids = [place_ref[k * tiles + tile, j] for j in range(listed)]
                key_rows = jnp.concatenate([k_pool[i] for i in ids], axis=0)
                scores = lax.dot_general(
                    q_refs[k][0, at, :], key_rows, (((1,), (1,)), ((), ())), preferred_element_type=F32
                )
                row_top = jnp.max(scores, axis=-1, keepdims=True)
                weights = jnp.exp2((scores - row_top) * factor)
                value_rows = jnp.concatenate([v_pool[i] for i in ids], axis=0)
                beside = jnp.concatenate([value_rows, jnp.ones_like(value_rows)], axis=1)
                mixed = jnp.dot(weights.astype(BF16), beside, preferred_element_type=F32)
                outs[k][0, at, :] = (mixed[:, :size] / mixed[:, size:]).astype(BF16)

    head_spec = pl.BlockSpec((1, rows, size), lambda h, _: (h, 0, 0))
    far_specs = [
        pl.BlockSpec((part.shape[0], 2, CAP, 1, TILE, size), lambda h, _: (0, 0, 0, h, 0, 0)) for part in far
    ]
    pool_size = near + sum(far_tiles)
    pairs = count * partners * tiles * listed
    return pl.pallas_call(
        kernel,
        grid_spec=pltpu.PrefetchScalarGridSpec(
            num_scalar_prefetch=1,
            grid=(count,),
            in_specs=[head_spec] * (3 * partners) + far_specs,
            out_specs=[head_spec] * partners,
            scratch_shapes=[pltpu.VMEM((pool_size, TILE, size), BF16)] * 2,
        ),
        out_shape=[jax.ShapeDtypeStruct((count, rows, size), BF16)] * partners,
        cost_estimate=pl.CostEstimate(
            flops=pairs * 4 * TILE * TILE * size,
            bytes_accessed=count * 2 * TILE * size * (2 * near + 2 * pool_size),
            transcendentals=pairs * TILE * TILE,
        ),
    )(places, *queries[::turn], *keys[::-1], *values, *far)


def plan(key_tiles, my_shard, here, shards, partners, tiles):
    shard_tiles = partners * tiles
    listed = key_tiles.shape[1]
    own = jnp.arange(shard_tiles, dtype=jnp.int32)
    place_of = ((own // tiles) ^ here) * tiles + own % tiles
    by_reader = key_tiles.reshape(shards, shard_tiles * listed)
    wanted = jnp.any(by_reader[:, :, None] == (my_shard * shard_tiles + own)[None, None, :], axis=1)
    rank = jnp.cumsum(wanted.astype(jnp.int32), axis=1) - 1
    slots = jnp.arange(CAP, dtype=jnp.int32)
    chosen = wanted[:, None, :] & (rank[:, None, :] == slots[None, :, None])
    picks = jnp.sum(jnp.where(chosen, place_of[None, None, :], 0), axis=2)
    lists = lax.dynamic_slice_in_dim(key_tiles, my_shard * shard_tiles, shard_tiles, 0)
    matches = lists[:, :, None] == jnp.arange(shards * shard_tiles, dtype=jnp.int32)[None, None, :]
    needed = jnp.any(matches, axis=(0, 1)).reshape(shards, shard_tiles)
    need_rank = jnp.cumsum(needed.astype(jnp.int32), axis=1) - 1
    far_at = jnp.arange(shards, dtype=jnp.int32)
    far_place = shard_tiles + far_at[:, None] * CAP + need_rank
    is_own = (jnp.arange(shards, dtype=jnp.int32) == my_shard)[:, None]
    place = jnp.where(is_own, place_of[None, :], far_place).reshape(-1)
    places = jnp.sum(jnp.where(matches, place[None, None, :], 0), axis=2)
    places = places.reshape(partners, tiles, listed)
    order = jnp.arange(partners, dtype=jnp.int32) ^ here
    places = jnp.take(places, order, axis=0).reshape(shard_tiles, listed)
    return picks.astype(jnp.int32), places.astype(jnp.int32)


def shards(queries, key_vectors, value_vectors, key_tiles):
    partners = lax.axis_size("head")
    shard_count = lax.axis_size("seq")
    here = lax.axis_index("head").astype(jnp.int32)
    my_shard = lax.axis_index("seq").astype(jnp.int32)
    here_arg = here.reshape(1)
    rows, heads, _ = queries.shape
    chunks = split_heads(heads // partners)
    tiles = rows // TILE

    def swap(piece, k):
        return piece if k == 0 else lax.ppermute(piece, "head", [(i, i ^ k) for i in range(partners)])

    def exchange(parts, c):
        return [swap(parts[k][c], k) for k in range(partners)]

    key_parts = by_partner(key_vectors, here_arg, partners, chunks)
    value_parts = by_partner(value_vectors, here_arg, partners, chunks)
    query_parts = by_partner(queries, here_arg, partners, chunks)
    picks, places = plan(key_tiles, my_shard, here, shard_count, partners, tiles)

    def share(keys, values):
        sent = pick_tiles(values, picks, 1, pick_tiles(keys, picks, 0, None))
        return [lax.all_to_all(sent, "seq", 0, 0, tiled=True)]

    picks, query_parts = lax.optimization_barrier((picks, query_parts))
    ready = []
    for c in range(len(chunks)):
        keys = exchange(key_parts, c)
        values = exchange(value_parts, c)
        ready.append((keys, values, share(keys, values)))
    asked = [exchange(query_parts, c) for c in range(len(chunks))]
    answers = []
    for c in range(len(chunks)):
        outs, _ = lax.optimization_barrier((attend(asked[c], *ready[c], places, -1 if c else 1), [pieces[-1] for pieces in asked]))
        answers.append([swap(outs[k], k) for k in range(partners)])
    return from_partners([[answers[c][k] for c in range(len(chunks))] for k in range(partners)], here_arg, chunks, heads)


def solution(mesh):
    return jax.shard_map(
        shards,
        mesh=mesh,
        in_specs=(
            P(("seq", "head"), None, None),
            P(("seq", "head"), None, None),
            P(("seq", "head"), None, None),
            P(),
        ),
        out_specs=P(("seq", "head"), None, None),
        check_vma=False,
    )
```

```python
import math

import jax
import jax.numpy as jnp
from jax import lax
from jax.experimental import pallas as pl
from jax.experimental.pallas import tpu as pltpu
from jax.sharding import PartitionSpec as P

TILE = 128
CAP = 2
CHUNKS = 2
BF16 = jnp.bfloat16
F32 = jnp.float32


def split_heads(own_heads):
    count = min(CHUNKS, own_heads)
    sizes = [own_heads // count + (i < own_heads % count) for i in range(count)]
    return [(sum(sizes[:i]), size) for i, size in enumerate(sizes)]


def row_block(rows):
    return TILE if rows % TILE == 0 else rows


def by_partner(array, here, partners, chunks):
    rows, heads, size = array.shape
    own_heads = heads // partners
    block = row_block(rows)

    def kernel(here_ref, in_ref, *refs):
        outs, turned = refs[:-1], refs[-1]
        turned[...] = jnp.swapaxes(in_ref[...], 0, 1)
        for k in range(partners):
            first = (here_ref[0] ^ k) * own_heads
            for c, (start, count) in enumerate(chunks):
                outs[k * len(chunks) + c][...] = turned[pl.ds(first + start, count)]

    parts = [count for _ in range(partners) for _, count in chunks]
    outs = pl.pallas_call(
        kernel,
        grid_spec=pltpu.PrefetchScalarGridSpec(
            num_scalar_prefetch=1,
            grid=(rows // block,),
            in_specs=[pl.BlockSpec((block, heads, size), lambda i, _: (i, 0, 0))],
            out_specs=[pl.BlockSpec((count, block, size), lambda i, _: (0, i, 0)) for count in parts],
            scratch_shapes=[pltpu.VMEM((heads, block, size), array.dtype)],
        ),
        out_shape=[jax.ShapeDtypeStruct((count, rows, size), array.dtype) for count in parts],
    )(here, array)
    return [outs[k * len(chunks) : (k + 1) * len(chunks)] for k in range(partners)]


def from_partners(pieces, here, chunks, heads):
    partners = len(pieces)
    own_heads = heads // partners
    rows, size = pieces[0][0].shape[1:]
    block = row_block(rows)

    def kernel(here_ref, *refs):
        ins, out, turned = refs[:-2], refs[-2], refs[-1]
        for k in range(partners):
            first = (here_ref[0] ^ k) * own_heads
            for c, (start, count) in enumerate(chunks):
                turned[pl.ds(first + start, count)] = ins[k * len(chunks) + c][...]
        out[...] = jnp.swapaxes(turned[...], 0, 1)

    flat = [piece for group in pieces for piece in group]
    return pl.pallas_call(
        kernel,
        grid_spec=pltpu.PrefetchScalarGridSpec(
            num_scalar_prefetch=1,
            grid=(rows // block,),
            in_specs=[pl.BlockSpec((piece.shape[0], block, size), lambda i, _: (0, i, 0)) for piece in flat],
            out_specs=pl.BlockSpec((block, heads, size), lambda i, _: (i, 0, 0)),
            scratch_shapes=[pltpu.VMEM((heads, block, size), BF16)],
        ),
        out_shape=jax.ShapeDtypeStruct((rows, heads, size), BF16),
        compiler_params=pltpu.CompilerParams(vmem_limit_bytes=16 * 2**20),
    )(here, *flat)


def pick_tiles(pieces, picks, kind, buffer):
    count, rows, size = pieces[0].shape
    readers = picks.shape[0]
    tiles = rows // TILE
    partners = len(pieces)

    def kernel(pick_ref, *refs):
        ins = refs[:partners][::-1]
        out, sems = refs[-2:]

        def copy_of(k, row, reader, slot):
            source = ins[k].at[:, pl.ds(row, TILE), :]
            return pltpu.make_async_copy(source, out.at[reader, kind, slot], sems.at[reader * CAP + slot])

        wanted = [(reader, slot) for reader in range(readers) for slot in range(CAP)]
        for reader, slot in wanted:
            place = pick_ref[reader, slot]
            row = pl.multiple_of(lax.rem(place, tiles) * TILE, TILE)
            for k in range(partners):

                @pl.when(lax.div(place, tiles) == k)
                def _(k=k, row=row, reader=reader, slot=slot):
                    copy_of(k, row, reader, slot).start()

        for reader, slot in wanted:
            copy_of(0, 0, reader, slot).wait()

    held = [] if buffer is None else [buffer]
    return pl.pallas_call(
        kernel,
        in_specs=[pl.BlockSpec(memory_space=pltpu.SMEM)]
        + [pl.BlockSpec(memory_space=pl.ANY)] * partners
        + [pl.BlockSpec(memory_space=pltpu.HBM)] * len(held),
        out_specs=pl.BlockSpec(memory_space=pltpu.HBM),
        scratch_shapes=[pltpu.SemaphoreType.DMA((readers * CAP,))],
        out_shape=jax.ShapeDtypeStruct((readers, 2, CAP, count, TILE, size), BF16),
        input_output_aliases={1 + partners: 0} if held else {},
        compiler_params=pltpu.CompilerParams(vmem_limit_bytes=50 * 2**20),
    )(picks, *pieces[::-1], *held)


def attend(queries, keys, values, far, places, orders):
    partners = len(queries)
    count, rows, size = queries[0].shape
    far_count = len(far)
    far_tiles = [part.shape[0] * CAP for part in far]
    tiles = rows // TILE
    near = partners * tiles
    listed = places.shape[1]
    factor = math.log2(math.e) / math.sqrt(size)

    def kernel(place_ref, *refs):
        q_refs, k_refs, v_refs = (
            [refs[i * partners + order.index(k)] for k in range(partners)] for i, order in enumerate(orders)
        )
        far_refs = refs[3 * partners : 3 * partners + far_count]
        outs, (k_pool, v_pool) = refs[3 * partners + far_count : -2], refs[-2:]
        for k in range(partners):
            k_pool[k * tiles : (k + 1) * tiles] = k_refs[k][0].reshape(tiles, TILE, size)
            v_pool[k * tiles : (k + 1) * tiles] = v_refs[k][0].reshape(tiles, TILE, size)
        place = near
        for k, many in enumerate(far_tiles):
            k_pool[place : place + many] = far_refs[k][:, 0, :, 0].reshape(many, TILE, size)
            v_pool[place : place + many] = far_refs[k][:, 1, :, 0].reshape(many, TILE, size)
            place += many
        for k in range(partners):
            for tile in range(tiles):
                at = pl.ds(tile * TILE, TILE)
                ids = [place_ref[k * tiles + tile, j] for j in range(listed)]
                key_rows = jnp.concatenate([k_pool[i] for i in ids], axis=0)
                scores = lax.dot_general(
                    q_refs[k][0, at, :], key_rows, (((1,), (1,)), ((), ())), preferred_element_type=F32
                )
                row_top = jnp.max(scores, axis=-1, keepdims=True)
                weights = jnp.exp2((scores - row_top) * factor)
                value_rows = jnp.concatenate([v_pool[i] for i in ids], axis=0)
                beside = jnp.concatenate([value_rows, jnp.ones_like(value_rows)], axis=1)
                mixed = jnp.dot(weights.astype(BF16), beside, preferred_element_type=F32)
                outs[k][0, at, :] = (mixed[:, :size] / mixed[:, size:]).astype(BF16)

    head_spec = pl.BlockSpec((1, rows, size), lambda h, _: (h, 0, 0))
    far_specs = [
        pl.BlockSpec((part.shape[0], 2, CAP, 1, TILE, size), lambda h, _: (0, 0, 0, h, 0, 0)) for part in far
    ]
    pool_size = near + sum(far_tiles)
    pairs = count * partners * tiles * listed
    return pl.pallas_call(
        kernel,
        grid_spec=pltpu.PrefetchScalarGridSpec(
            num_scalar_prefetch=1,
            grid=(count,),
            in_specs=[head_spec] * (3 * partners) + far_specs,
            out_specs=[head_spec] * partners,
            scratch_shapes=[pltpu.VMEM((pool_size, TILE, size), BF16)] * 2,
        ),
        out_shape=[jax.ShapeDtypeStruct((count, rows, size), BF16)] * partners,
        compiler_params=pltpu.CompilerParams(vmem_limit_bytes=50 * 2**20),
        cost_estimate=pl.CostEstimate(
            flops=pairs * 4 * TILE * TILE * size,
            bytes_accessed=count * 2 * TILE * size * (2 * near + 2 * pool_size),
            transcendentals=pairs * TILE * TILE,
        ),
    )(places, *(side[k] for side, order in zip((queries, keys, values), orders) for k in order), *far)


def orders_of(partners, c):
    up = list(range(partners))
    down = up[::-1]
    return [down if c else up, down, up]


def plan(key_tiles, my_shard, here, shards, partners, tiles):
    shard_tiles = partners * tiles
    listed = key_tiles.shape[1]
    own = jnp.arange(shard_tiles, dtype=jnp.int32)
    place_of = ((own // tiles) ^ here) * tiles + own % tiles
    by_reader = key_tiles.reshape(shards, shard_tiles * listed)
    wanted = jnp.any(by_reader[:, :, None] == (my_shard * shard_tiles + own)[None, None, :], axis=1)
    rank = jnp.cumsum(wanted.astype(jnp.int32), axis=1) - 1
    slots = jnp.arange(CAP, dtype=jnp.int32)
    chosen = wanted[:, None, :] & (rank[:, None, :] == slots[None, :, None])
    picks = jnp.sum(jnp.where(chosen, place_of[None, None, :], 0), axis=2)
    lists = lax.dynamic_slice_in_dim(key_tiles, my_shard * shard_tiles, shard_tiles, 0)
    matches = lists[:, :, None] == jnp.arange(shards * shard_tiles, dtype=jnp.int32)[None, None, :]
    needed = jnp.any(matches, axis=(0, 1)).reshape(shards, shard_tiles)
    need_rank = jnp.cumsum(needed.astype(jnp.int32), axis=1) - 1
    far_at = jnp.arange(shards, dtype=jnp.int32)
    far_place = shard_tiles + far_at[:, None] * CAP + need_rank
    is_own = (jnp.arange(shards, dtype=jnp.int32) == my_shard)[:, None]
    place = jnp.where(is_own, place_of[None, :], far_place).reshape(-1)
    places = jnp.sum(jnp.where(matches, place[None, None, :], 0), axis=2)
    places = places.reshape(partners, tiles, listed)
    order = jnp.arange(partners, dtype=jnp.int32) ^ here
    places = jnp.take(places, order, axis=0).reshape(shard_tiles, listed)
    return picks.astype(jnp.int32), places.astype(jnp.int32)


def shards(queries, key_vectors, value_vectors, key_tiles):
    partners = lax.axis_size("head")
    shard_count = lax.axis_size("seq")
    here = lax.axis_index("head").astype(jnp.int32)
    my_shard = lax.axis_index("seq").astype(jnp.int32)
    here_arg = here.reshape(1)
    rows, heads, _ = queries.shape
    chunks = split_heads(heads // partners)
    tiles = rows // TILE

    def swap(piece, k):
        return piece if k == 0 else lax.ppermute(piece, "head", [(i, i ^ k) for i in range(partners)])

    def exchange(parts, c):
        return [swap(parts[k][c], k) for k in range(partners)]

    key_parts = by_partner(key_vectors, here_arg, partners, chunks)
    value_parts = by_partner(value_vectors, here_arg, partners, chunks)
    query_parts = by_partner(queries, here_arg, partners, chunks)
    picks, places = plan(key_tiles, my_shard, here, shard_count, partners, tiles)

    def share(keys, values):
        sent = pick_tiles(values, picks, 1, pick_tiles(keys, picks, 0, None))
        return [lax.all_to_all(sent, "seq", 0, 0, tiled=True)]

    picks, query_parts = lax.optimization_barrier((picks, query_parts))
    ready = []
    for c in range(len(chunks)):
        keys = exchange(key_parts, c)
        values = exchange(value_parts, c)
        ready.append((keys, values, share(keys, values)))
    asked = [exchange(query_parts, c) for c in range(len(chunks))]
    answers = []
    for c in range(len(chunks)):
        outs, _ = lax.optimization_barrier((attend(asked[c], *ready[c], places, orders_of(partners, c)), [pieces[-1] for pieces in asked]))
        answers.append([swap(outs[k], k) for k in range(partners)])
    return from_partners([[answers[c][k] for c in range(len(chunks))] for k in range(partners)], here_arg, chunks, heads)


def solution(mesh):
    return jax.shard_map(
        shards,
        mesh=mesh,
        in_specs=(
            P(("seq", "head"), None, None),
            P(("seq", "head"), None, None),
            P(("seq", "head"), None, None),
            P(),
        ),
        out_specs=P(("seq", "head"), None, None),
        check_vma=False,
    )
```

```python
import math

import jax
import jax.numpy as jnp
from jax import lax
from jax.experimental import pallas as pl
from jax.experimental.pallas import tpu as pltpu
from jax.sharding import PartitionSpec as P

TILE = 128
CAP = 2
CHUNKS = 2
AHEAD = 2
BF16 = jnp.bfloat16
F32 = jnp.float32


def split_heads(own_heads):
    count = min(CHUNKS, own_heads)
    sizes = [own_heads // count + (i < own_heads % count) for i in range(count)]
    return [(sum(sizes[:i]), size) for i, size in enumerate(sizes)]


def row_block(rows):
    return TILE if rows % TILE == 0 else rows


def by_partner(array, here, partners, cuts):
    rows, heads, size = array.shape
    own_heads = heads // partners
    block = row_block(rows)

    def kernel(here_ref, in_ref, *refs):
        outs, turned = refs[:-1], refs[-1]
        turned[...] = jnp.swapaxes(in_ref[...], 0, 1)
        at = 0
        for k in range(partners):
            first = (here_ref[0] ^ k) * own_heads
            for start, count in cuts[k]:
                outs[at][...] = turned[pl.ds(first + start, count)]
                at += 1

    parts = [count for cut in cuts for _, count in cut]
    outs = pl.pallas_call(
        kernel,
        grid_spec=pltpu.PrefetchScalarGridSpec(
            num_scalar_prefetch=1,
            grid=(rows // block,),
            in_specs=[pl.BlockSpec((block, heads, size), lambda i, _: (i, 0, 0))],
            out_specs=[pl.BlockSpec((count, block, size), lambda i, _: (0, i, 0)) for count in parts],
            scratch_shapes=[pltpu.VMEM((heads, block, size), array.dtype)],
        ),
        out_shape=[jax.ShapeDtypeStruct((count, rows, size), array.dtype) for count in parts],
    )(here, array)
    outs = iter(outs)
    return [[next(outs) for _ in cut] for cut in cuts]


def from_partners(pieces, here, chunks, heads):
    partners = len(pieces)
    own_heads = heads // partners
    rows, size = pieces[0][0].shape[1:]
    block = row_block(rows)

    def kernel(here_ref, *refs):
        ins, out, turned = refs[:-2], refs[-2], refs[-1]
        for k in range(partners):
            first = (here_ref[0] ^ k) * own_heads
            for c, (start, count) in enumerate(chunks):
                turned[pl.ds(first + start, count)] = ins[k * len(chunks) + c][...]
        out[...] = jnp.swapaxes(turned[...], 0, 1)

    flat = [piece for group in pieces for piece in group]
    return pl.pallas_call(
        kernel,
        grid_spec=pltpu.PrefetchScalarGridSpec(
            num_scalar_prefetch=1,
            grid=(rows // block,),
            in_specs=[pl.BlockSpec((piece.shape[0], block, size), lambda i, _: (0, i, 0)) for piece in flat],
            out_specs=pl.BlockSpec((block, heads, size), lambda i, _: (i, 0, 0)),
            scratch_shapes=[pltpu.VMEM((heads, block, size), BF16)],
        ),
        out_shape=jax.ShapeDtypeStruct((rows, heads, size), BF16),
        compiler_params=pltpu.CompilerParams(vmem_limit_bytes=16 * 2**20),
    )(here, *flat)


def pick_tiles(pieces, picks, kind, buffer):
    count, rows, size = pieces[0].shape
    readers = picks.shape[0]
    tiles = rows // TILE
    partners = len(pieces)

    def kernel(pick_ref, *refs):
        ins = refs[:partners][::-1]
        out, sems = refs[-2:]

        def copy_of(k, row, reader, slot):
            source = ins[k].at[:, pl.ds(row, TILE), :]
            return pltpu.make_async_copy(source, out.at[reader, kind, slot], sems.at[reader * CAP + slot])

        wanted = [(reader, slot) for reader in range(readers) for slot in range(CAP)]
        for reader, slot in wanted:
            place = pick_ref[reader, slot]
            row = pl.multiple_of(lax.rem(place, tiles) * TILE, TILE)
            for k in range(partners):

                @pl.when(lax.div(place, tiles) == k)
                def _(k=k, row=row, reader=reader, slot=slot):
                    copy_of(k, row, reader, slot).start()

        for reader, slot in wanted:
            copy_of(0, 0, reader, slot).wait()

    held = [] if buffer is None else [buffer]
    return pl.pallas_call(
        kernel,
        in_specs=[pl.BlockSpec(memory_space=pltpu.SMEM)]
        + [pl.BlockSpec(memory_space=pl.ANY)] * partners
        + [pl.BlockSpec(memory_space=pltpu.HBM)] * len(held),
        out_specs=pl.BlockSpec(memory_space=pltpu.HBM),
        scratch_shapes=[pltpu.SemaphoreType.DMA((readers * CAP,))],
        out_shape=jax.ShapeDtypeStruct((readers, 2, CAP, count, TILE, size), BF16),
        input_output_aliases={1 + partners: 0} if held else {},
        compiler_params=pltpu.CompilerParams(vmem_limit_bytes=50 * 2**20),
    )(picks, *pieces[::-1], *held)


def attend(queries, keys, values, far, places, orders):
    partners = len(queries)
    count, rows, size = keys[0].shape
    rest = list(queries[-1][1:])
    first = queries[-1][0].shape[0]
    far_count = len(far)
    far_tiles = [part.shape[0] * CAP for part in far]
    tiles = rows // TILE
    near = partners * tiles
    listed = places.shape[1]
    factor = math.log2(math.e) / math.sqrt(size)

    def kernel(place_ref, *refs):
        late, refs = refs[: len(rest)], refs[len(rest) :]
        q_refs, k_refs, v_refs = (
            [refs[i * partners + order.index(k)] for k in range(partners)] for i, order in enumerate(orders)
        )
        in_late = pl.program_id(0) >= first

        def query_of(k, at):
            if k < partners - 1 or not late:
                return q_refs[k][0, at, :]
            return jnp.where(in_late, late[0][0, at, :], q_refs[k][0, at, :])

        far_refs = refs[3 * partners : 3 * partners + far_count]
        outs, (k_pool, v_pool) = refs[3 * partners + far_count : -2], refs[-2:]
        for k in range(partners):
            k_pool[k * tiles : (k + 1) * tiles] = k_refs[k][0].reshape(tiles, TILE, size)
            v_pool[k * tiles : (k + 1) * tiles] = v_refs[k][0].reshape(tiles, TILE, size)
        place = near
        for k, many in enumerate(far_tiles):
            k_pool[place : place + many] = far_refs[k][:, 0, :, 0].reshape(many, TILE, size)
            v_pool[place : place + many] = far_refs[k][:, 1, :, 0].reshape(many, TILE, size)
            place += many
        for k in range(partners):
            for tile in range(tiles):
                at = pl.ds(tile * TILE, TILE)
                ids = [place_ref[k * tiles + tile, j] for j in range(listed)]
                key_rows = jnp.concatenate([k_pool[i] for i in ids], axis=0)
                scores = lax.dot_general(
                    query_of(k, at), key_rows, (((1,), (1,)), ((), ())), preferred_element_type=F32
                )
                row_top = jnp.max(scores, axis=-1, keepdims=True)
                weights = jnp.exp2((scores - row_top) * factor)
                value_rows = jnp.concatenate([v_pool[i] for i in ids], axis=0)
                beside = jnp.concatenate([value_rows, jnp.ones_like(value_rows)], axis=1)
                mixed = jnp.dot(weights.astype(BF16), beside, preferred_element_type=F32)
                outs[k][0, at, :] = (mixed[:, :size] / mixed[:, size:]).astype(BF16)

    head_spec = pl.BlockSpec((1, rows, size), lambda h, _: (h, 0, 0))
    first_spec = pl.BlockSpec((1, rows, size), lambda h, _: (jnp.minimum(h, first - 1), 0, 0))
    rest_spec = pl.BlockSpec((1, rows, size), lambda h, _: (jnp.maximum(h - first, 0), 0, 0))
    far_specs = [
        pl.BlockSpec((part.shape[0], 2, CAP, 1, TILE, size), lambda h, _: (0, 0, 0, h, 0, 0)) for part in far
    ]
    pool_size = near + sum(far_tiles)
    pairs = count * partners * tiles * listed
    return pl.pallas_call(
        kernel,
        grid_spec=pltpu.PrefetchScalarGridSpec(
            num_scalar_prefetch=1,
            grid=(count,),
            in_specs=[rest_spec] * len(rest)
            + [first_spec if k == partners - 1 else head_spec for k in orders[0]]
            + [head_spec] * (2 * partners)
            + far_specs,
            out_specs=[head_spec] * partners,
            scratch_shapes=[pltpu.VMEM((pool_size, TILE, size), BF16)] * 2,
        ),
        out_shape=[jax.ShapeDtypeStruct((count, rows, size), BF16)] * partners,
        compiler_params=pltpu.CompilerParams(vmem_limit_bytes=50 * 2**20),
        cost_estimate=pl.CostEstimate(
            flops=pairs * 4 * TILE * TILE * size,
            bytes_accessed=count * 2 * TILE * size * (2 * near + 2 * pool_size),
            transcendentals=pairs * TILE * TILE,
        ),
    )(
        places,
        *rest,
        *(side[k] for side, order in zip(([part[0] for part in queries], keys, values), orders) for k in order),
        *far,
    )


def orders_of(partners, c):
    up = list(range(partners))
    down = up[::-1]
    return [down if c else up, down, up]


def plan(key_tiles, my_shard, here, shards, partners, tiles):
    shard_tiles = partners * tiles
    listed = key_tiles.shape[1]
    own = jnp.arange(shard_tiles, dtype=jnp.int32)
    place_of = ((own // tiles) ^ here) * tiles + own % tiles
    by_reader = key_tiles.reshape(shards, shard_tiles * listed)
    wanted = jnp.any(by_reader[:, :, None] == (my_shard * shard_tiles + own)[None, None, :], axis=1)
    rank = jnp.cumsum(wanted.astype(jnp.int32), axis=1) - 1
    slots = jnp.arange(CAP, dtype=jnp.int32)
    chosen = wanted[:, None, :] & (rank[:, None, :] == slots[None, :, None])
    picks = jnp.sum(jnp.where(chosen, place_of[None, None, :], 0), axis=2)
    lists = lax.dynamic_slice_in_dim(key_tiles, my_shard * shard_tiles, shard_tiles, 0)
    matches = lists[:, :, None] == jnp.arange(shards * shard_tiles, dtype=jnp.int32)[None, None, :]
    needed = jnp.any(matches, axis=(0, 1)).reshape(shards, shard_tiles)
    need_rank = jnp.cumsum(needed.astype(jnp.int32), axis=1) - 1
    far_at = jnp.arange(shards, dtype=jnp.int32)
    far_place = shard_tiles + far_at[:, None] * CAP + need_rank
    is_own = (jnp.arange(shards, dtype=jnp.int32) == my_shard)[:, None]
    place = jnp.where(is_own, place_of[None, :], far_place).reshape(-1)
    places = jnp.sum(jnp.where(matches, place[None, None, :], 0), axis=2)
    places = places.reshape(partners, tiles, listed)
    order = jnp.arange(partners, dtype=jnp.int32) ^ here
    places = jnp.take(places, order, axis=0).reshape(shard_tiles, listed)
    return picks.astype(jnp.int32), places.astype(jnp.int32)


def shards(queries, key_vectors, value_vectors, key_tiles):
    partners = lax.axis_size("head")
    shard_count = lax.axis_size("seq")
    here = lax.axis_index("head").astype(jnp.int32)
    my_shard = lax.axis_index("seq").astype(jnp.int32)
    here_arg = here.reshape(1)
    rows, heads, _ = queries.shape
    chunks = split_heads(heads // partners)
    tiles = rows // TILE

    def swap(piece, k):
        return piece if k == 0 else lax.ppermute(piece, "head", [(i, i ^ k) for i in range(partners)])

    def exchange(parts, c):
        return [swap(parts[k][c], k) for k in range(partners)]

    cuts = [chunks] * partners
    key_parts = by_partner(key_vectors, here_arg, partners, cuts)
    value_parts = by_partner(value_vectors, here_arg, partners, cuts)
    start, count = chunks[-1]
    ahead = max(1, count * AHEAD // 5)
    query_cuts = cuts[:-1] + [chunks[:-1] + [(start, ahead), (start + ahead, count - ahead)]]
    query_parts = by_partner(queries, here_arg, partners, query_cuts)
    picks, places = plan(key_tiles, my_shard, here, shard_count, partners, tiles)
    picks, query_parts = lax.optimization_barrier((picks, query_parts))

    held = [(exchange(key_parts, c), exchange(value_parts, c)) for c in range(len(chunks))]
    asked = [[[swap(query_parts[k][c], k)] for k in range(partners)] for c in range(len(chunks) - 1)]
    asked.append([[swap(query_parts[k][len(chunks) - 1], k)] for k in range(partners - 1)])
    early, _ = lax.optimization_barrier((query_parts[-1][-2], held[0][0][-1]))
    early = swap(early, partners - 1)
    asked[-1].append([early, swap(query_parts[-1][-1], partners - 1)])

    def share(c):
        keys, values = held[c]
        sent = pick_tiles(values, picks, 1, pick_tiles(keys, picks, 0, None))
        if c == 0:
            sent, _ = lax.optimization_barrier((sent, early))
        return [lax.all_to_all(sent, "seq", 0, 0, tiled=True)]

    far = [share(c) for c in range(len(chunks))]
    answers = []
    for c in range(len(chunks)):
        outs = attend(asked[c], *held[c], far[c], places, orders_of(partners, c))
        outs, _ = lax.optimization_barrier((outs, [pieces[-1][-1] for pieces in asked]))
        answers.append([swap(outs[k], k) for k in range(partners)])
    return from_partners([[answers[c][k] for c in range(len(chunks))] for k in range(partners)], here_arg, chunks, heads)


def solution(mesh):
    return jax.shard_map(
        shards,
        mesh=mesh,
        in_specs=(
            P(("seq", "head"), None, None),
            P(("seq", "head"), None, None),
            P(("seq", "head"), None, None),
            P(),
        ),
        out_specs=P(("seq", "head"), None, None),
        check_vma=False,
    )
```

```python
import math

import jax
import jax.numpy as jnp
from jax import lax
from jax.experimental import pallas as pl
from jax.experimental.pallas import tpu as pltpu
from jax.sharding import PartitionSpec as P

TILE = 128
CAP = 2
CHUNKS = 2
AHEAD = 2
BF16 = jnp.bfloat16
F32 = jnp.float32


def split_heads(own_heads):
    count = min(CHUNKS, own_heads)
    sizes = [own_heads // count + (i < own_heads % count) for i in range(count)]
    return [(sum(sizes[:i]), size) for i, size in enumerate(sizes)]


def row_block(rows):
    return TILE if rows % TILE == 0 else rows


def by_partner(array, here, partners, cuts):
    rows, heads, size = array.shape
    own_heads = heads // partners
    block = row_block(rows)

    def kernel(here_ref, in_ref, *refs):
        outs, turned = refs[:-1], refs[-1]
        turned[...] = jnp.swapaxes(in_ref[...], 0, 1)
        at = 0
        for k in range(partners):
            first = (here_ref[0] ^ k) * own_heads
            for start, count in cuts[k]:
                outs[at][...] = turned[pl.ds(first + start, count)]
                at += 1

    parts = [count for cut in cuts for _, count in cut]
    outs = pl.pallas_call(
        kernel,
        grid_spec=pltpu.PrefetchScalarGridSpec(
            num_scalar_prefetch=1,
            grid=(rows // block,),
            in_specs=[pl.BlockSpec((block, heads, size), lambda i, _: (i, 0, 0))],
            out_specs=[pl.BlockSpec((count, block, size), lambda i, _: (0, i, 0)) for count in parts],
            scratch_shapes=[pltpu.VMEM((heads, block, size), array.dtype)],
        ),
        out_shape=[jax.ShapeDtypeStruct((count, rows, size), array.dtype) for count in parts],
    )(here, array)
    outs = iter(outs)
    return [[next(outs) for _ in cut] for cut in cuts]


def from_partners(pieces, here, chunks, heads):
    partners = len(pieces)
    own_heads = heads // partners
    rows, size = pieces[0][0].shape[1:]
    block = row_block(rows)

    def kernel(here_ref, *refs):
        ins, out, turned = refs[:-2], refs[-2], refs[-1]
        for k in range(partners):
            first = (here_ref[0] ^ k) * own_heads
            for c, (start, count) in enumerate(chunks):
                turned[pl.ds(first + start, count)] = ins[k * len(chunks) + c][...]
        out[...] = jnp.swapaxes(turned[...], 0, 1)

    flat = [piece for group in pieces for piece in group]
    return pl.pallas_call(
        kernel,
        grid_spec=pltpu.PrefetchScalarGridSpec(
            num_scalar_prefetch=1,
            grid=(rows // block,),
            in_specs=[pl.BlockSpec((piece.shape[0], block, size), lambda i, _: (0, i, 0)) for piece in flat],
            out_specs=pl.BlockSpec((block, heads, size), lambda i, _: (i, 0, 0)),
            scratch_shapes=[pltpu.VMEM((heads, block, size), BF16)],
        ),
        out_shape=jax.ShapeDtypeStruct((rows, heads, size), BF16),
        compiler_params=pltpu.CompilerParams(vmem_limit_bytes=16 * 2**20),
    )(here, *flat)


def pick_tiles(pieces, picks, kind, buffer):
    count, rows, size = pieces[0].shape
    readers = picks.shape[0]
    tiles = rows // TILE
    partners = len(pieces)

    def kernel(pick_ref, *refs):
        ins = refs[:partners][::-1]
        out, sems = refs[-2:]

        def copy_of(k, row, reader, slot):
            source = ins[k].at[:, pl.ds(row, TILE), :]
            return pltpu.make_async_copy(source, out.at[reader, kind, slot], sems.at[reader * CAP + slot])

        wanted = [(reader, slot) for reader in range(readers) for slot in range(CAP)]
        for reader, slot in wanted:
            place = pick_ref[reader, slot]
            row = pl.multiple_of(lax.rem(place, tiles) * TILE, TILE)
            for k in range(partners):

                @pl.when(lax.div(place, tiles) == k)
                def _(k=k, row=row, reader=reader, slot=slot):
                    copy_of(k, row, reader, slot).start()

        for reader, slot in wanted:
            copy_of(0, 0, reader, slot).wait()

    held = [] if buffer is None else [buffer]
    return pl.pallas_call(
        kernel,
        in_specs=[pl.BlockSpec(memory_space=pltpu.SMEM)]
        + [pl.BlockSpec(memory_space=pl.ANY)] * partners
        + [pl.BlockSpec(memory_space=pltpu.HBM)] * len(held),
        out_specs=pl.BlockSpec(memory_space=pltpu.HBM),
        scratch_shapes=[pltpu.SemaphoreType.DMA((readers * CAP,))],
        out_shape=jax.ShapeDtypeStruct((readers, 2, CAP, count, TILE, size), BF16),
        input_output_aliases={1 + partners: 0} if held else {},
        compiler_params=pltpu.CompilerParams(vmem_limit_bytes=50 * 2**20),
    )(picks, *pieces[::-1], *held)


def attend(queries, keys, values, far, places, orders):
    partners = len(queries)
    count, rows, size = keys[0].shape
    rest = list(queries[-1][1:])
    first = queries[-1][0].shape[0]
    far_count = len(far)
    far_tiles = [part.shape[0] * CAP for part in far]
    tiles = rows // TILE
    near = partners * tiles
    listed = places.shape[1]
    factor = math.log2(math.e) / math.sqrt(size)

    def kernel(place_ref, *refs):
        late, refs = refs[: len(rest)], refs[len(rest) :]
        q_refs, k_refs, v_refs = (
            [refs[i * partners + order.index(k)] for k in range(partners)] for i, order in enumerate(orders)
        )
        in_late = pl.program_id(0) >= first

        def query_of(k, at):
            if k < partners - 1 or not late:
                return q_refs[k][0, at, :]
            return jnp.where(in_late, late[0][0, at, :], q_refs[k][0, at, :])

        far_refs = refs[3 * partners : 3 * partners + far_count]
        outs, (k_pool, v_pool) = refs[3 * partners + far_count : -2], refs[-2:]
        for k in range(partners):
            k_pool[k * tiles : (k + 1) * tiles] = k_refs[k][0].reshape(tiles, TILE, size)
            v_pool[k * tiles : (k + 1) * tiles] = v_refs[k][0].reshape(tiles, TILE, size)
        place = near
        for k, many in enumerate(far_tiles):
            k_pool[place : place + many] = far_refs[k][:, 0, :, 0].reshape(many, TILE, size)
            v_pool[place : place + many] = far_refs[k][:, 1, :, 0].reshape(many, TILE, size)
            place += many
        for k in range(partners):
            for tile in range(tiles):
                at = pl.ds(tile * TILE, TILE)
                ids = [place_ref[k * tiles + tile, j] for j in range(listed)]
                key_rows = jnp.concatenate([k_pool[i] for i in ids], axis=0)
                scores = lax.dot_general(
                    query_of(k, at), key_rows, (((1,), (1,)), ((), ())), preferred_element_type=F32
                )
                row_top = jnp.max(scores, axis=-1, keepdims=True)
                weights = jnp.exp2((scores - row_top) * factor)
                value_rows = jnp.concatenate([v_pool[i] for i in ids], axis=0)
                beside = jnp.concatenate([value_rows, jnp.ones_like(value_rows)], axis=1)
                mixed = jnp.dot(weights.astype(BF16), beside, preferred_element_type=F32)
                outs[k][0, at, :] = (mixed[:, :size] / mixed[:, size:]).astype(BF16)

    head_spec = pl.BlockSpec((1, rows, size), lambda h, _: (h, 0, 0))
    first_spec = pl.BlockSpec((1, rows, size), lambda h, _: (jnp.minimum(h, first - 1), 0, 0))
    rest_spec = pl.BlockSpec((1, rows, size), lambda h, _: (jnp.maximum(h - first, 0), 0, 0))
    far_specs = [
        pl.BlockSpec((part.shape[0], 2, CAP, 1, TILE, size), lambda h, _: (0, 0, 0, h, 0, 0)) for part in far
    ]
    pool_size = near + sum(far_tiles)
    pairs = count * partners * tiles * listed
    return pl.pallas_call(
        kernel,
        grid_spec=pltpu.PrefetchScalarGridSpec(
            num_scalar_prefetch=1,
            grid=(count,),
            in_specs=[rest_spec] * len(rest)
            + [first_spec if k == partners - 1 else head_spec for k in orders[0]]
            + [head_spec] * (2 * partners)
            + far_specs,
            out_specs=[head_spec] * partners,
            scratch_shapes=[pltpu.VMEM((pool_size, TILE, size), BF16)] * 2,
        ),
        out_shape=[jax.ShapeDtypeStruct((count, rows, size), BF16)] * partners,
        compiler_params=pltpu.CompilerParams(vmem_limit_bytes=50 * 2**20),
        cost_estimate=pl.CostEstimate(
            flops=pairs * 4 * TILE * TILE * size,
            bytes_accessed=count * 2 * TILE * size * (2 * near + 2 * pool_size),
            transcendentals=pairs * TILE * TILE,
        ),
    )(
        places,
        *rest,
        *(side[k] for side, order in zip(([part[0] for part in queries], keys, values), orders) for k in order),
        *far,
    )


def orders_of(partners, c):
    up = list(range(partners))
    down = up[::-1]
    return [down if c else up, down, up]


def plan(key_tiles, my_shard, here, shards, partners, tiles):
    shard_tiles = partners * tiles
    listed = key_tiles.shape[1]
    own = jnp.arange(shard_tiles, dtype=jnp.int32)
    place_of = ((own // tiles) ^ here) * tiles + own % tiles
    by_reader = key_tiles.reshape(shards, shard_tiles * listed)
    wanted = jnp.any(by_reader[:, :, None] == (my_shard * shard_tiles + own)[None, None, :], axis=1)
    rank = jnp.cumsum(wanted.astype(jnp.int32), axis=1) - 1
    slots = jnp.arange(CAP, dtype=jnp.int32)
    chosen = wanted[:, None, :] & (rank[:, None, :] == slots[None, :, None])
    picks = jnp.sum(jnp.where(chosen, place_of[None, None, :], 0), axis=2)
    lists = lax.dynamic_slice_in_dim(key_tiles, my_shard * shard_tiles, shard_tiles, 0)
    matches = lists[:, :, None] == jnp.arange(shards * shard_tiles, dtype=jnp.int32)[None, None, :]
    needed = jnp.any(matches, axis=(0, 1)).reshape(shards, shard_tiles)
    need_rank = jnp.cumsum(needed.astype(jnp.int32), axis=1) - 1
    far_at = jnp.arange(shards, dtype=jnp.int32)
    far_place = shard_tiles + far_at[:, None] * CAP + need_rank
    is_own = (jnp.arange(shards, dtype=jnp.int32) == my_shard)[:, None]
    place = jnp.where(is_own, place_of[None, :], far_place).reshape(-1)
    places = jnp.sum(jnp.where(matches, place[None, None, :], 0), axis=2)
    places = places.reshape(partners, tiles, listed)
    order = jnp.arange(partners, dtype=jnp.int32) ^ here
    places = jnp.take(places, order, axis=0).reshape(shard_tiles, listed)
    return picks.astype(jnp.int32), places.astype(jnp.int32)


def shards(queries, key_vectors, value_vectors, key_tiles):
    partners = lax.axis_size("head")
    shard_count = lax.axis_size("seq")
    here = lax.axis_index("head").astype(jnp.int32)
    my_shard = lax.axis_index("seq").astype(jnp.int32)
    here_arg = here.reshape(1)
    rows, heads, _ = queries.shape
    chunks = split_heads(heads // partners)
    tiles = rows // TILE

    def swap(piece, k):
        return piece if k == 0 else lax.ppermute(piece, "head", [(i, i ^ k) for i in range(partners)])

    def exchange(parts, c):
        return [swap(parts[k][c], k) for k in range(partners)]

    cuts = [chunks] * partners
    key_parts = by_partner(key_vectors, here_arg, partners, cuts)
    value_parts = by_partner(value_vectors, here_arg, partners, cuts)
    start, count = chunks[-1]
    ahead = max(1, count * AHEAD // 5)
    query_cuts = cuts[:-1] + [chunks[:-1] + [(start, ahead), (start + ahead, count - ahead)]]
    query_parts = by_partner(queries, here_arg, partners, query_cuts)
    picks, places = plan(key_tiles, my_shard, here, shard_count, partners, tiles)
    picks, query_parts = lax.optimization_barrier((picks, query_parts))

    held = [(exchange(key_parts, c), exchange(value_parts, c)) for c in range(len(chunks))]
    asked = [[[swap(query_parts[k][c], k)] for k in range(partners)] for c in range(len(chunks) - 1)]
    asked.append([[swap(query_parts[k][len(chunks) - 1], k)] for k in range(partners - 1)])
    early, _ = lax.optimization_barrier((query_parts[-1][-2], held[0][0][-1]))
    early = swap(early, partners - 1)
    asked[-1].append([early, swap(query_parts[-1][-1], partners - 1)])

    def share(c):
        keys, values = held[c]
        sent = pick_tiles(values, picks, 1, pick_tiles(keys, picks, 0, None))
        if c == 0:
            sent, _ = lax.optimization_barrier((sent, early))
        return [lax.all_to_all(sent, "seq", 0, 0, tiled=True)]

    far = [share(c) for c in range(len(chunks))]
    answers = []
    for c in range(len(chunks)):
        outs = attend(asked[c], *held[c], far[c], places, orders_of(partners, c))
        outs, _ = lax.optimization_barrier((outs, [pieces[-1][-1] for pieces in asked] + [asked[0][1][0]]))
        answers.append([swap(outs[k], k) for k in range(partners)])
    return from_partners([[answers[c][k] for c in range(len(chunks))] for k in range(partners)], here_arg, chunks, heads)


def solution(mesh):
    return jax.shard_map(
        shards,
        mesh=mesh,
        in_specs=(
            P(("seq", "head"), None, None),
            P(("seq", "head"), None, None),
            P(("seq", "head"), None, None),
            P(),
        ),
        out_specs=P(("seq", "head"), None, None),
        check_vma=False,
    )
```
